128 devices in a mesh: chan: 32 (over x, z, y_lo), tm: 4 (over y_hi, core).
Axes of the slice: x: 4, y: 4 (y_hi: 2, y_lo: 2; y = y_hi * 2 + y_lo), z: 4, core: 2. Of those that a mesh axis runs over, the one named last changes fastest.
Arguments:
- samples: bfloat16 [4096, 98304], P('chan', 'tm'), may hold values from -6 to 6
- plan: int32 [3], replicated, may hold values from 0 to 31
- owner_table: int32 [32], replicated, may hold values from 0 to 31, each once
Outputs:
- correlations: float32 [128, 3, 101, 4096], P('tm', None, None, 'chan')
The draws below stay inside these ranges and needn't reach their ends.
Inputs may be any that keep to these rules, and one draw needn't show every extreme that they name: `plan`: each entry names a cable block. `owner_table`: each stored block holds exactly one cable block.
All inputs are finite; a program needn't handle non-finite values.
Results may differ from the reference program's by a relative error of at most 0.0036.
Values may be sent and summed in bfloat16 or wider, within the bound.
No kernel may reach another device: no remote copies, remote signals or barrier semaphores. Data moves between devices by JAX's collectives and lax.ppermute only.
A program may use at most 128 MiB of HBM per device.

```python
import math
import jax
import jax.numpy as jnp
from jax import lax

CHAN_DEV = 128
WINLEN = 1024
BINS = 128
BIN0 = 16
SMOOTH = 4
LAGS = 101
STEPS = 3
CHANNELS = 4096
WINDOWS = 192
SAMPLES = 98304
N_CHAN = 32


def level_of(rng, dims, split, least, largest):
    level, own = 1.0, jax.random.fold_in(rng, 6)
    for dim, shards_of in split:
        heights = jnp.exp(jax.random.uniform(jax.random.fold_in(own, dim), (shards_of,), jnp.float32, least / len(split), largest / len(split)))
        level = level * jnp.repeat(heights, dims[dim] // shards_of).reshape([-1 if axis == dim else 1 for axis in range(len(dims))])
    return level


def noise(rng, dims, deviation, most, shards=(), kind=jnp.bfloat16):
    drawn = jax.random.normal(rng, dims, jnp.float32) * deviation
    if len(shards) > 0:
        drawn = level_of(rng, dims, shards, -0.22, 0.18) * drawn
    return jnp.clip(drawn, min=-most, max=most).astype(kind)


def setup_inputs(seed: int = 0) -> dict:
    seeds = jax.random.split(jax.random.key(seed), 4)
    return {
        "samples": noise(seeds[0], (CHANNELS, SAMPLES), 1.0, 6.0, ((0, 32), (1, 4))),
        "plan": jax.random.randint(seeds[1], (STEPS,), 0, N_CHAN).astype(jnp.int32),
        "owner_table": jax.random.permutation(seeds[2], N_CHAN).astype(jnp.int32),
    }


magnitude_eps = 1e-06
water_level = 0.25

def dft_table():
    positions = jnp.arange(WINLEN, dtype=jnp.int32)
    bin_index = BIN0 + jnp.arange(BINS, dtype=jnp.int32)
    phase_steps = positions[:, None] * bin_index[None, :] % WINLEN
    angles = 2.0 * math.pi / WINLEN * phase_steps.astype(jnp.float32)
    taper = 0.5 - 0.5 * jnp.cos(2.0 * math.pi / WINLEN * positions.astype(jnp.float32))
    return jnp.concatenate([taper[:, None] * jnp.cos(angles), -taper[:, None] * jnp.sin(angles)], axis=1).astype(jnp.bfloat16)

def band_table():
    bin_index = jnp.arange(BINS, dtype=jnp.int32)
    inside = (jnp.abs(bin_index[:, None] - bin_index[None, :]) <= SMOOTH).astype(jnp.float32)
    totals = lax.optimization_barrier(jnp.sum(inside, axis=0))
    return inside / totals[None, :]

def lag_table(windows):
    lag_steps = jnp.arange(LAGS, dtype=jnp.int32) - LAGS // 2
    bin_index = BIN0 + jnp.arange(BINS, dtype=jnp.int32)
    phase_steps = jnp.mod(lag_steps[:, None] * bin_index[None, :], WINLEN)
    angles = 2.0 * math.pi / WINLEN * phase_steps.astype(jnp.float32)
    factor = 1.0 / math.sqrt(BINS * windows)
    return jnp.stack([jnp.cos(angles) * factor, -jnp.sin(angles) * factor], axis=1)

def whiten(spectra, band):
    real_part = spectra[..., :BINS]
    imag_part = spectra[..., BINS:]
    magnitude = jnp.sqrt(real_part * real_part + imag_part * imag_part + magnitude_eps)
    running = jnp.dot(magnitude.reshape(-1, BINS), band, precision=lax.Precision.HIGHEST).reshape(magnitude.shape)
    divisor = running + water_level * lax.optimization_barrier(jnp.mean(magnitude, axis=-1, keepdims=True))
    return (spectra / jnp.concatenate([divisor, divisor], axis=-1)).astype(jnp.bfloat16)

def cross_spectra(own_rows, reference_rows):
    own_parts = own_rows.astype(jnp.float32).reshape(own_rows.shape[0], own_rows.shape[1], 2, BINS)
    ref_parts = reference_rows.astype(jnp.float32).reshape(reference_rows.shape[0], reference_rows.shape[1], 2, BINS)
    rotated = jnp.stack([-ref_parts[:, :, 1], ref_parts[:, :, 0]], axis=2)
    real_part = jnp.einsum('awkf,bwkf->fba', own_parts, ref_parts, precision=lax.Precision.HIGHEST)
    imag_part = jnp.einsum('awkf,bwkf->fba', own_parts, rotated, precision=lax.Precision.HIGHEST)
    return jnp.stack([real_part, imag_part])

def reference(samples, plan, owner_table):
    hop_len = WINLEN // 2
    transform = dft_table()
    band = band_table()
    lag_weights = lag_table(WINDOWS)
    blocks = samples.reshape(N_CHAN, CHAN_DEV, SAMPLES)

    def block_spectra(block_rows):
        hop_rows = block_rows.reshape(CHAN_DEV, WINDOWS, hop_len)
        padded = jnp.concatenate([hop_rows, jnp.zeros((CHAN_DEV, 1, hop_len), jnp.bfloat16)], axis=1)
        frames = jnp.concatenate([padded[:, :-1], padded[:, 1:]], axis=2)
        spectra = jnp.dot(frames.reshape(-1, WINLEN), transform, preferred_element_type=jnp.float32)
        return whiten(spectra.reshape(CHAN_DEV, WINDOWS, 2 * BINS), band)
    whitened = lax.map(block_spectra, blocks)
    results = []
    for step_index in range(STEPS):
        root_index = owner_table[plan[step_index]].astype(jnp.int32)
        reference_rows = lax.dynamic_index_in_dim(whitened, root_index, 0, keepdims=False)

        def block_lags(own_rows):
            spectra_pair = cross_spectra(own_rows, reference_rows)
            return jnp.einsum('tkf,kfba->bta', lag_weights, spectra_pair, precision=lax.Precision.HIGHEST)
        lagged = lax.map(block_lags, whitened)
        results.append(jnp.transpose(lagged, (1, 2, 0, 3)).reshape(CHAN_DEV, LAGS, CHANNELS))
    return jnp.stack(results, axis=1)
```

```python
import functools
import math

import jax
import jax.numpy as jnp
import ml_dtypes
import numpy as np
from jax import lax
from jax.experimental import pallas as pl
from jax.experimental.pallas import tpu as pltpu
from jax.sharding import PartitionSpec as P

WINLEN = 1024
HOP = 512
BINS = 128
BIN0 = 16
SMOOTH = 4
LAGS = 101
STEPS = 3
HALF_RANK = 24
RANK = 2 * HALF_RANK
ROW = 136
magnitude_eps = 1e-06
water_level = 0.25
VMEM_BYTES = 60 * 1024 * 1024


def dft_table():
    n = np.arange(WINLEN)
    k = BIN0 + np.arange(BINS)
    angles = 2.0 * math.pi / WINLEN * (k[:, None] * n[None, :] % WINLEN)
    taper = 0.5 - 0.5 * np.cos(2.0 * math.pi / WINLEN * n)
    table = np.concatenate([np.cos(angles) * taper, -np.sin(angles) * taper], axis=0)
    return table.astype(np.float32).astype(ml_dtypes.bfloat16)


def band_tables():
    f = np.arange(BINS)
    inside = (np.abs(f[:, None] - f[None, :]) <= SMOOTH).astype(np.float32)
    counts = inside.sum(axis=1)
    return np.tile(inside, (1, 3)).astype(ml_dtypes.bfloat16), (1.0 / counts)[:, None].astype(np.float32)


def dot(a, b):
    return math.fsum(p * q for p, q in zip(a, b))


def row_basis(rows, count):
    left = [list(r) for r in rows]
    basis = []
    for _ in range(count):
        norms = [dot(r, r) for r in left]
        best = max(range(len(left)), key=lambda i: norms[i])
        q = left[best]
        for _ in range(2):
            for b in basis:
                d = dot(q, b)
                q = [x - d * y for x, y in zip(q, b)]
            size = math.sqrt(dot(q, q))
            q = [x / size for x in q]
        basis.append(q)
        for i, r in enumerate(left):
            d = dot(r, q)
            left[i] = [x - d * y for x, y in zip(r, q)]
    return basis


@functools.cache
def lag_factors(windows):
    factor = 1.0 / math.sqrt(BINS * windows)
    mid = LAGS // 2
    bins = range(BIN0, BIN0 + BINS)

    def angle(tau, k):
        return 2.0 * math.pi / WINLEN * (tau * k % WINLEN)

    even = [[math.cos(angle(t, k)) for k in bins] for t in range(mid + 1)]
    odd = [[-math.sin(angle(t, k)) for k in bins] for t in range(1, mid + 1)]
    even_basis = row_basis(even, HALF_RANK)
    odd_basis = row_basis(odd, HALF_RANK)
    even_u = np.array([[dot(r, b) for b in even_basis] for r in even])
    odd_u = np.array([[dot(r, b) for b in odd_basis] for r in odd])
    u = np.zeros((LAGS, RANK))
    for t in range(LAGS):
        tau = t - mid
        u[t, :HALF_RANK] = even_u[abs(tau)]
        if tau:
            u[t, HALF_RANK:] = math.copysign(1.0, tau) * odd_u[abs(tau) - 1]
    return u * factor, np.array(even_basis), np.array(odd_basis)


def split_bf16(value):
    high = value.astype(np.float32).astype(ml_dtypes.bfloat16)
    low = (value - high.astype(np.float64)).astype(np.float32).astype(ml_dtypes.bfloat16)
    return high, low


def bin_order():
    order = []
    for j in range(32):
        x, z, y = j // 8, j // 2 % 4, j % 2
        order += [2 * j, 2 * j + 1]
        order += [64 + 2 * ((z * 4 + x) * 2 + y), 65 + 2 * ((z * 4 + x) * 2 + y)]
    return np.array(order)


def spectra_kernel(windows, chunk, x_ref, next_ref, edge_ref, table_ref, band_ref, inverse_ref, out_ref, rows):
    i = pl.program_id(0)
    last = pl.num_programs(0) - 1
    tail = jnp.where(i == last, edge_ref[...], next_ref[...])
    for pair in range(chunk // 2):
        frames = []
        for w in (2 * pair, 2 * pair + 1):
            if w == chunk - 1:
                frames.append(jnp.concatenate([x_ref[:, w * HOP :], tail], axis=1))
            else:
                frames.append(x_ref[:, w * HOP : w * HOP + WINLEN])
        spectra = lax.dot_general(
            table_ref[...],
            jnp.concatenate(frames, axis=0),
            (((1,), (1,)), ((), ())),
            preferred_element_type=jnp.float32,
        )
        re, im = spectra[:BINS], spectra[BINS:]
        magnitude = jnp.sqrt(re * re + im * im + magnitude_eps)
        high = magnitude.astype(jnp.bfloat16)
        rest = magnitude - high.astype(jnp.float32)
        mid = rest.astype(jnp.bfloat16)
        low = (rest - mid.astype(jnp.float32)).astype(jnp.bfloat16)
        running = jnp.dot(
            band_ref[...], jnp.concatenate([high, mid, low], axis=0), preferred_element_type=jnp.float32
        )
        mean = jnp.sum(magnitude, axis=0, keepdims=True) * (1.0 / BINS)
        scale = 1.0 / (running * inverse_ref[...] + water_level * mean)
        for part, value in enumerate((re, im)):
            white = value * scale
            for h in range(2):
                row = part * windows + i * chunk + 2 * pair + h
                rows[pl.ds(row, BINS, stride=2 * windows), :] = white[:, h * 128 : (h + 1) * 128]

    @pl.when(i == last)
    def _():
        def one(j, carry):
            x, z, y = j // 8, (j // 2) % 4, j % 2
            first = 2 * j
            second = 64 + 2 * ((z * 4 + x) * 2 + y)
            for slot, f in enumerate((first, first + 1, second, second + 1)):
                start = pl.multiple_of(f * 2 * windows, 2 * windows)
                out_ref[4 * j + slot] = rows[pl.ds(start, 2 * windows), :].astype(jnp.bfloat16)
            return carry

        lax.fori_loop(0, 32, one, 0)


def whitened_spectra(samples, edge):
    channels, length = samples.shape
    windows = length // HOP
    chunk = 8
    band, inverse = band_tables()
    steps = windows // chunk
    whole = lambda shape: pl.BlockSpec(shape, lambda i: (0,) * len(shape))
    return pl.pallas_call(
        functools.partial(spectra_kernel, windows, chunk),
        grid=(steps,),
        out_shape=jax.ShapeDtypeStruct((BINS, 2 * windows, channels), jnp.bfloat16),
        in_specs=[
            pl.BlockSpec((channels, chunk * HOP), lambda i: (0, i)),
            pl.BlockSpec((channels, HOP), lambda i: (0, jnp.minimum((i + 1) * chunk, windows - 1))),
            whole((channels, HOP)),
            whole((2 * BINS, WINLEN)),
            whole((BINS, 3 * BINS)),
            whole((BINS, 1)),
        ],
        out_specs=whole((BINS, 2 * windows, channels)),
        scratch_shapes=[pltpu.VMEM((BINS * 2 * windows, channels), jnp.float32)],
        compiler_params=pltpu.CompilerParams(vmem_limit_bytes=VMEM_BYTES),
        name="spectra",
    )(samples, samples, edge, jnp.asarray(dft_table()), jnp.asarray(band), jnp.asarray(inverse))


def cross_kernel(windows, sizes, slots_ref, v_ref, own_ref, *refs):
    pieces = refs[: len(sizes)]
    out_ref, real_rows, imag_rows = refs[len(sizes) :]
    base = 0
    for piece, size in zip(pieces, sizes):

        def one(n, carry, piece=piece, base=base):
            q = slots_ref[base + n]
            own = own_ref[q]
            turned = jnp.concatenate([own[windows:], -own[:windows]], axis=0)
            cross = lax.dot_general(
                piece[n],
                jnp.concatenate([own, turned], axis=1),
                (((0,), (0,)), ((), ())),
                preferred_element_type=jnp.float32,
            )
            real_rows[pl.ds(q, 128, stride=ROW), :] = cross[:, :128]
            imag_rows[pl.ds(q, 128, stride=ROW), :] = cross[:, 128:]
            return carry

        lax.fori_loop(0, size, one, 0, unroll=4)
        base += size

    def two(n, carry):
        halves = []
        for h in range(2):
            start = pl.multiple_of((2 * n + h) * ROW, 8)
            halves.append(
                jnp.concatenate(
                    [real_rows[pl.ds(start, 128), :], imag_rows[pl.ds(start, 128), :]], axis=0
                ).astype(jnp.bfloat16)
            )
        both = jnp.dot(v_ref[...], jnp.concatenate(halves, axis=1), preferred_element_type=jnp.float32)
        total = both[:RANK] + both[RANK:]
        for h in range(2):
            out_ref[2 * n + h] = total[:, h * 128 : (h + 1) * 128].astype(out_ref.dtype)
        return carry

    lax.fori_loop(0, 64, two, 0, unroll=2)


def lag_coefficients(own, pieces, slots, v):
    windows = own.shape[1] // 2
    sizes = tuple(p.shape[0] for p in pieces)
    vmem = pl.BlockSpec(memory_space=pltpu.VMEM)
    return pl.pallas_call(
        functools.partial(cross_kernel, windows, sizes),
        out_shape=jax.ShapeDtypeStruct((128, RANK, 128), jnp.bfloat16),
        in_specs=[pl.BlockSpec(memory_space=pltpu.SMEM)] + [vmem] * (2 + len(pieces)),
        out_specs=vmem,
        scratch_shapes=[pltpu.VMEM((128 * ROW, 128), jnp.float32)] * 2,
        compiler_params=pltpu.CompilerParams(vmem_limit_bytes=VMEM_BYTES),
        name="cross",
    )(slots, v, own, *pieces)


def expand_kernel(u_ref, *refs):
    coefs, out_ref = refs[:-1], refs[-1]
    for s, c_ref in enumerate(coefs):

        def two(n, carry, s=s, c_ref=c_ref):
            value = jnp.concatenate([c_ref[2 * n], c_ref[2 * n + 1]], axis=1)
            high = value.astype(jnp.bfloat16)
            low = (value - high.astype(jnp.float32)).astype(jnp.bfloat16)
            lags = jnp.dot(
                u_ref[...], jnp.concatenate([high, high, low], axis=0), preferred_element_type=jnp.float32
            )
            out_ref[2 * n, s] = lags[:LAGS, :128]
            out_ref[2 * n + 1, s] = lags[:LAGS, 128:]
            return carry

        lax.fori_loop(0, c_ref.shape[0] // 2, two, 0, unroll=2)


def expand(coefs, u):
    vmem = pl.BlockSpec(memory_space=pltpu.VMEM)
    return pl.pallas_call(
        expand_kernel,
        out_shape=jax.ShapeDtypeStruct((coefs[0].shape[0], len(coefs), LAGS, 128), jnp.float32),
        in_specs=[vmem] * (1 + len(coefs)),
        out_specs=vmem,
        compiler_params=pltpu.CompilerParams(vmem_limit_bytes=VMEM_BYTES),
        name="expand",
    )(u, *coefs)


def place(x, z, y):
    return (x % 4) * 8 + (z % 4) * 2 + y % 2


def shift(value, dx=0, dz=0, dy=0):
    pairs = [(place(x, z, y), place(x + dx, z + dz, y + dy)) for x in range(4) for z in range(4) for y in range(2)]
    return lax.ppermute(value, "chan", pairs)


def gather_references(parts):
    both = jnp.concatenate([parts, shift(parts, dy=1)], axis=1)
    first = jnp.concatenate([both[:, 0:2], both[:, 4:6]], axis=1)
    second = jnp.concatenate([both[:, 2:4], both[:, 6:8]], axis=1)
    a = [shift(first, dz=1), shift(first, dz=-1)]
    b = [shift(second, dx=1), shift(second, dx=-1)]
    a, b = lax.optimization_barrier((a, b))
    a += [shift(a[0][:, :2], dz=1), shift(a[1][:, 2:], dz=-1)]
    b += [shift(b[0][:, :2], dx=1), shift(b[1][:, 2:], dx=-1)]
    a, b = lax.optimization_barrier((a, b))
    plane_a = jnp.concatenate([first] + a, axis=1)
    plane_b = jnp.concatenate([second] + b, axis=1)
    steps = parts.shape[0]
    before = None
    for s in range(steps + 1):
        sends = []
        for plane, axis in ((plane_a, "dx"), (plane_b, "dz")):
            for side, sign in ((0, 1), (1, -1)):
                group = []
                if before is not None:
                    got = before[axis][side]
                    group.append(got[:8] if side == 0 else got[8:])
                if s < steps:
                    group.append(plane[s])
                value = jnp.concatenate(group, axis=0) if len(group) > 1 else group[0]
                sends.append(shift(value, **{axis: sign}))
        sends = lax.optimization_barrier(sends)
        ahead = {}
        far = {}
        for n, axis in enumerate(("dx", "dz")):
            pair = sends[2 * n : 2 * n + 2]
            if before is not None:
                far[axis] = [p[:8] for p in pair]
                pair = [p[8:] for p in pair]
            ahead[axis] = pair
        if before is not None:
            yield (
                [plane_a[s - 1]] + before["dx"] + far["dx"] + [plane_b[s - 1]] + before["dz"] + far["dz"]
            )
        before = ahead


def slot_table():
    me = lax.axis_index("chan")
    x, z, y = me // 8, me // 2 % 4, me % 2
    offsets = (0, -1, 1, 2)
    dl, ds, dy, e = np.meshgrid(np.array(offsets), np.array(offsets), np.arange(2), np.arange(2), indexing="ij")
    dl, ds, dy, e = (t.reshape(-1).astype(np.int32) for t in (dl, ds, dy, e))
    y_of = (y + dy) % 2
    first = (((x + dl + 4) % 4) * 8 + ((z + ds + 4) % 4) * 2 + y_of) * 4 + e
    second = (((x + ds + 4) % 4) * 8 + ((z + dl + 4) % 4) * 2 + y_of) * 4 + 2 + e
    return jnp.concatenate([first, second]).astype(jnp.int32)


def sum_over_spans(value):
    me = lax.axis_index("tm")
    half, core = me // 2, me % 2
    quarters = value.reshape(2, 2, 32, RANK, 128)
    sent = lax.dynamic_index_in_dim(quarters, 1 - core, 1, keepdims=False)
    kept = lax.dynamic_index_in_dim(quarters, core, 1, keepdims=False).astype(jnp.float32)
    got = lax.ppermute(sent, "tm", [(0, 1), (1, 0), (2, 3), (3, 2)])
    chip = kept + got.astype(jnp.float32)
    sent = lax.dynamic_index_in_dim(chip, 1 - half, 0, keepdims=False).astype(jnp.bfloat16)
    kept = lax.dynamic_index_in_dim(chip, half, 0, keepdims=False)
    got = lax.ppermute(sent, "tm", [(0, 2), (2, 0), (1, 3), (3, 1)])
    return kept + got.astype(jnp.float32)


def shards(samples, plan, owner_table):
    windows = samples.shape[1] // HOP * lax.axis_size("tm")
    edge = lax.ppermute(samples[:, :HOP], "tm", [(1, 0), (2, 1), (3, 2)])
    own = whitened_spectra(samples, edge)
    everyone = lax.all_to_all(own.reshape((32, 4) + own.shape[1:]), "chan", 0, 0)
    roots = owner_table[plan]
    parts = jnp.stack([lax.dynamic_index_in_dim(everyone, roots[s], 0, keepdims=False) for s in range(STEPS)])
    u, even_basis, odd_basis = lag_factors(windows)
    order = bin_order()
    v = np.zeros((RANK, 2 * BINS))
    v[:HALF_RANK, :BINS] = even_basis[:, order]
    v[HALF_RANK:, BINS:] = odd_basis[:, order]
    v = jnp.asarray(np.concatenate(split_bf16(v), axis=0))
    padded = np.zeros((104, RANK))
    padded[:LAGS] = u
    u_high, u_low = split_bf16(padded)
    u = jnp.asarray(np.concatenate([u_high, u_low, u_high], axis=1))
    slots = slot_table()
    totals = []
    for pieces in gather_references(parts):
        totals.append(sum_over_spans(lag_coefficients(own, pieces, slots, v)))
    return expand(totals, u)


def solution(mesh):
    placed = (P("chan", "tm"), P(), P())
    return jax.shard_map(
        shards, mesh=mesh, in_specs=placed, out_specs=P("tm", None, None, "chan"), check_vma=False
    )
```

```python
import functools
import math

import jax
import jax.numpy as jnp
import ml_dtypes
import numpy as np
from jax import lax
from jax.experimental import pallas as pl
from jax.experimental.pallas import tpu as pltpu
from jax.sharding import PartitionSpec as P

WINLEN = 1024
HOP = 512
BINS = 128
BIN0 = 16
SMOOTH = 4
LAGS = 101
STEPS = 3
HALF_RANK = 24
RANK = 2 * HALF_RANK
ROW = 136
GROUP = 8
magnitude_eps = 1e-06
water_level = 0.25
VMEM_BYTES = 60 * 1024 * 1024


def dft_table():
    n = np.arange(WINLEN)
    k = BIN0 + np.arange(BINS)
    angles = 2.0 * math.pi / WINLEN * (k[:, None] * n[None, :] % WINLEN)
    taper = 0.5 - 0.5 * np.cos(2.0 * math.pi / WINLEN * n)
    table = np.concatenate([np.cos(angles) * taper, -np.sin(angles) * taper], axis=0)
    return table.astype(np.float32).astype(ml_dtypes.bfloat16)


def band_tables():
    f = np.arange(BINS)
    inside = (np.abs(f[:, None] - f[None, :]) <= SMOOTH).astype(np.float32)
    counts = inside.sum(axis=1)
    return np.tile(inside, (1, 2)).astype(ml_dtypes.bfloat16), (1.0 / counts)[:, None].astype(np.float32)


def dot(a, b):
    return math.fsum(p * q for p, q in zip(a, b))


def row_basis(rows, count):
    left = [list(r) for r in rows]
    basis = []
    for _ in range(count):
        norms = [dot(r, r) for r in left]
        best = max(range(len(left)), key=lambda i: norms[i])
        q = left[best]
        for _ in range(2):
            for b in basis:
                d = dot(q, b)
                q = [x - d * y for x, y in zip(q, b)]
            size = math.sqrt(dot(q, q))
            q = [x / size for x in q]
        basis.append(q)
        for i, r in enumerate(left):
            d = dot(r, q)
            left[i] = [x - d * y for x, y in zip(r, q)]
    return basis


@functools.cache
def lag_factors(windows):
    factor = 1.0 / math.sqrt(BINS * windows)
    mid = LAGS // 2
    bins = range(BIN0, BIN0 + BINS)

    def angle(tau, k):
        return 2.0 * math.pi / WINLEN * (tau * k % WINLEN)

    even = [[math.cos(angle(t, k)) for k in bins] for t in range(mid + 1)]
    odd = [[-math.sin(angle(t, k)) for k in bins] for t in range(1, mid + 1)]
    even_basis = row_basis(even, HALF_RANK)
    odd_basis = row_basis(odd, HALF_RANK)
    even_u = np.array([[dot(r, b) for b in even_basis] for r in even])
    odd_u = np.array([[dot(r, b) for b in odd_basis] for r in odd])
    u = np.zeros((LAGS, RANK))
    for t in range(LAGS):
        tau = t - mid
        u[t, :HALF_RANK] = even_u[abs(tau)]
        if tau:
            u[t, HALF_RANK:] = math.copysign(1.0, tau) * odd_u[abs(tau) - 1]
    return u * factor, np.array(even_basis), np.array(odd_basis)


def split_bf16(value):
    high = value.astype(np.float32).astype(ml_dtypes.bfloat16)
    low = (value - high.astype(np.float64)).astype(np.float32).astype(ml_dtypes.bfloat16)
    return high, low


def bin_order():
    order = []
    for j in range(32):
        x, z, y = j // 8, j // 2 % 4, j % 2
        order += [2 * j, 2 * j + 1]
        order += [64 + 2 * ((z * 4 + x) * 2 + y), 65 + 2 * ((z * 4 + x) * 2 + y)]
    return np.array(order)


def spectra_kernel(chunk, x_ref, next_ref, edge_ref, table_ref, band_ref, inverse_ref, out_ref, rows):
    i = pl.program_id(0)
    tail = jnp.where(i == pl.num_programs(0) - 1, edge_ref[...], next_ref[...])
    pairs = range(chunk // 2)
    spectra, magnitudes, parts = [], [], []
    for pair in pairs:
        frames = []
        for w in (2 * pair, 2 * pair + 1):
            if w == chunk - 1:
                frames.append(jnp.concatenate([x_ref[:, w * HOP :], tail], axis=1))
            else:
                frames.append(x_ref[:, w * HOP : w * HOP + WINLEN])
        spectra.append(
            lax.dot_general(
                table_ref[...],
                jnp.concatenate(frames, axis=0),
                (((1,), (1,)), ((), ())),
                preferred_element_type=jnp.float32,
            )
        )
    for value in spectra:
        re, im = value[:BINS], value[BINS:]
        magnitude = jnp.sqrt(re * re + im * im + magnitude_eps)
        high = magnitude.astype(jnp.bfloat16)
        low = (magnitude - high.astype(jnp.float32)).astype(jnp.bfloat16)
        magnitudes.append(magnitude)
        parts.append(jnp.concatenate([high, low], axis=0))
    totals = [jnp.dot(band_ref[...], p, preferred_element_type=jnp.float32) for p in parts]
    for pair in pairs:
        mean = jnp.sum(magnitudes[pair], axis=0, keepdims=True) * (1.0 / BINS)
        scale = 1.0 / (totals[pair] * inverse_ref[...] + water_level * mean)
        for part in range(2):
            white = spectra[pair][part * BINS : (part + 1) * BINS] * scale
            for h in range(2):
                row = part * chunk + 2 * pair + h
                rows[pl.ds(row, BINS, stride=2 * chunk), :] = white[:, h * 128 : (h + 1) * 128]
    for q, f in enumerate(bin_order()):
        out_ref[q] = rows[2 * chunk * int(f) : 2 * chunk * (int(f) + 1), :].astype(jnp.bfloat16)


def whitened_spectra(samples, edge):
    channels, length = samples.shape
    windows = length // HOP
    band, inverse = band_tables()
    whole = lambda shape: pl.BlockSpec(shape, lambda i: (0,) * len(shape))
    return pl.pallas_call(
        functools.partial(spectra_kernel, GROUP),
        grid=(windows // GROUP,),
        out_shape=jax.ShapeDtypeStruct((BINS, 2 * windows, channels), jnp.bfloat16),
        in_specs=[
            pl.BlockSpec((channels, GROUP * HOP), lambda i: (0, i)),
            pl.BlockSpec((channels, HOP), lambda i: (0, jnp.minimum((i + 1) * GROUP, windows - 1))),
            whole((channels, HOP)),
            whole((2 * BINS, WINLEN)),
            whole((BINS, 2 * BINS)),
            whole((BINS, 1)),
        ],
        out_specs=pl.BlockSpec((BINS, 2 * GROUP, channels), lambda i: (0, i, 0)),
        scratch_shapes=[pltpu.VMEM((BINS * 2 * GROUP, channels), jnp.float32)],
        compiler_params=pltpu.CompilerParams(vmem_limit_bytes=VMEM_BYTES),
        name="spectra",
    )(samples, samples, edge, jnp.asarray(dft_table()), jnp.asarray(band), jnp.asarray(inverse))


def cross_kernel(count, slots_ref, v_ref, own_hbm, *refs):
    pieces = refs[:count]
    keep_ref, send_ref, own_ref, other_ref, real_rows, imag_rows, sems, own_sem = refs[count:]
    size = BINS // count
    own_copy = pltpu.make_async_copy(own_hbm, own_ref, own_sem)
    own_copy.start()
    for i, piece in enumerate(pieces):
        pltpu.make_async_copy(piece, other_ref.at[pl.ds(size * i, size)], sems.at[i]).start()
    own_copy.wait()
    per = 32 // size

    def one(k, carry):
        for i in range(per):
            landed = other_ref.at[pl.ds(size * (k * per + i), size)]
            pltpu.make_async_copy(landed, landed, sems.at[k * per + i]).wait()
        results = []
        for j in range(32):
            n = k * 32 + j
            own = own_ref[slots_ref[n]]
            turned = []
            for r in range(0, own.shape[0], 2 * GROUP):
                turned += [own[r + GROUP : r + 2 * GROUP], -own[r : r + GROUP]]
            results.append(
                lax.dot_general(
                    other_ref[n],
                    jnp.concatenate([own, jnp.concatenate(turned, axis=0)], axis=1),
                    (((0,), (0,)), ((), ())),
                    preferred_element_type=jnp.float32,
                )
            )
        for j, cross in enumerate(results):
            real_rows[pl.ds(k * 32 + j, 128, stride=ROW), :] = cross[:, :128]
            imag_rows[pl.ds(k * 32 + j, 128, stride=ROW), :] = cross[:, 128:]
        return carry

    lax.fori_loop(0, BINS // 32, one, 0)
    core = slots_ref[BINS]
    for out_ref, which in ((send_ref, 1 - core), (keep_ref, core)):

        def two(h, carry, out_ref=out_ref, which=which):
            results = []
            for j in range(16):
                halves = []
                for e in range(2):
                    start = pl.multiple_of((h * 64 + which * 32 + 2 * j + e) * ROW, 8)
                    halves.append(
                        jnp.concatenate(
                            [real_rows[pl.ds(start, 128), :], imag_rows[pl.ds(start, 128), :]], axis=0
                        ).astype(jnp.bfloat16)
                    )
                results.append(
                    jnp.dot(v_ref[...], jnp.concatenate(halves, axis=1), preferred_element_type=jnp.float32)
                )
            for j, both in enumerate(results):
                total = (both[:RANK] + both[RANK:]).astype(out_ref.dtype)
                out_ref[h, 2 * j] = total[:, :128]
                out_ref[h, 2 * j + 1] = total[:, 128:]
            return carry

        lax.fori_loop(0, 2, two, 0)


def lag_coefficients(own, pieces, slots, v):
    vmem = pl.BlockSpec(memory_space=pltpu.VMEM)
    hbm = pl.BlockSpec(memory_space=pl.ANY)
    rows = (2, 32, RANK, 128)
    return pl.pallas_call(
        functools.partial(cross_kernel, len(pieces)),
        out_shape=[jax.ShapeDtypeStruct(rows, jnp.float32), jax.ShapeDtypeStruct(rows, jnp.bfloat16)],
        in_specs=[pl.BlockSpec(memory_space=pltpu.SMEM), vmem] + [hbm] * (1 + len(pieces)),
        out_specs=[vmem, vmem],
        scratch_shapes=[pltpu.VMEM(own.shape, jnp.bfloat16)] * 2
        + [pltpu.VMEM((128 * ROW, 128), jnp.float32)] * 2
        + [pltpu.SemaphoreType.DMA((len(pieces),)), pltpu.SemaphoreType.DMA],
        compiler_params=pltpu.CompilerParams(vmem_limit_bytes=VMEM_BYTES),
        name="cross",
    )(slots, v, own, *pieces)


def expand_kernel(step, u_ref, kept_ref, got_ref, *refs):
    out_ref, lags_ref, sem = refs[-3:]
    count = kept_ref.shape[0]
    results = []
    for n in range(0, count, 2):
        value = jnp.concatenate(
            [kept_ref[b] + got_ref[b].astype(jnp.float32) for b in (n, n + 1)], axis=1
        )
        high = value.astype(jnp.bfloat16)
        low = (value - high.astype(jnp.float32)).astype(jnp.bfloat16)
        results.append(
            jnp.dot(u_ref[...], jnp.concatenate([high, high, low], axis=0), preferred_element_type=jnp.float32)
        )
    for n, lags in enumerate(results):
        lags_ref[pl.ds(2 * n, LAGS, stride=count), :] = lags[:LAGS, :128]
        lags_ref[pl.ds(2 * n + 1, LAGS, stride=count), :] = lags[:LAGS, 128:]
    copy = pltpu.make_async_copy(lags_ref, out_ref.at[step], sem)
    copy.start()
    copy.wait()


def expand(step, u, kept, got, before):
    vmem = pl.BlockSpec(memory_space=pltpu.VMEM)
    hbm = pl.BlockSpec(memory_space=pl.ANY)
    shape = (LAGS * kept.shape[0], 128)
    held = [] if before is None else [before]
    return pl.pallas_call(
        functools.partial(expand_kernel, step),
        out_shape=jax.ShapeDtypeStruct((STEPS,) + shape, jnp.float32),
        in_specs=[vmem] * 3 + [hbm] * len(held),
        out_specs=hbm,
        scratch_shapes=[pltpu.VMEM(shape, jnp.float32), pltpu.SemaphoreType.DMA],
        input_output_aliases={3: 0} if held else {},
        compiler_params=pltpu.CompilerParams(vmem_limit_bytes=VMEM_BYTES),
        name="expand",
    )(u, kept, got, *held)


def place(x, z, y):
    return (x % 4) * 8 + (z % 4) * 2 + y % 2


def shift(value, dx=0, dz=0, dy=0):
    pairs = [(place(x, z, y), place(x + dx, z + dz, y + dy)) for x in range(4) for z in range(4) for y in range(2)]
    return lax.ppermute(value, "chan", pairs)


def around(value, axis):
    return [value] + [shift(value, **{axis: step}) for step in (1, -1, 2)]


def gather_references(parts):
    other = shift(parts, dy=1)
    first = jnp.concatenate([parts[:, :2], other[:, :2]], axis=1)
    second = jnp.concatenate([parts[:, 2:], other[:, 2:]], axis=1)
    plane_a = jnp.concatenate(around(first, "dz"), axis=1)
    plane_b = jnp.concatenate(around(second, "dx"), axis=1)
    return [around(plane_a[s], "dx") + around(plane_b[s], "dz") for s in range(parts.shape[0])]


def slot_table():
    me = lax.axis_index("chan")
    x, z, y = me // 8, me // 2 % 4, me % 2
    offsets = np.array((0, -1, 1, 2))
    last, plane, dy, e = np.meshgrid(offsets, offsets, np.arange(2), np.arange(2), indexing="ij")
    last, plane, dy, e = (t.reshape(-1).astype(np.int32) for t in (last, plane, dy, e))
    y_of = (y + dy) % 2
    first = (((x + last + 4) % 4) * 8 + ((z + plane + 4) % 4) * 2 + y_of) * 4 + e
    second = (((x + plane + 4) % 4) * 8 + ((z + last + 4) % 4) * 2 + y_of) * 4 + 2 + e
    return jnp.concatenate([first, second]).astype(jnp.int32)


def sum_over_spans(keep, send):
    half = lax.axis_index("tm") // 2
    got = lax.ppermute(send, "tm", [(0, 1), (1, 0), (2, 3), (3, 2)])

    def chip(which):
        own = lax.dynamic_index_in_dim(keep, which, 0, keepdims=False)
        return own + lax.dynamic_index_in_dim(got, which, 0, keepdims=False).astype(jnp.float32)

    far = lax.ppermute(chip(1 - half).astype(jnp.bfloat16), "tm", [(0, 2), (2, 0), (1, 3), (3, 1)])
    return chip(half), far


def basis_columns(windows, slots):
    _, even, odd = lag_factors(windows)
    parts = [split_bf16(t[:, bin_order()]) for t in (even, odd)]
    table = np.concatenate([parts[0][0], parts[1][0], parts[0][1], parts[1][1]], axis=0)
    chosen = (jnp.arange(BINS, dtype=jnp.int32)[:, None] == slots[None, :]).astype(jnp.bfloat16)
    table = jnp.dot(jnp.asarray(table), chosen, preferred_element_type=jnp.float32).astype(jnp.bfloat16)
    is_odd = (np.arange(2 * RANK) // HALF_RANK % 2 == 1)[:, None]
    nothing = jnp.zeros_like(table)
    return jnp.concatenate([jnp.where(is_odd, nothing, table), jnp.where(is_odd, table, nothing)], axis=1)


def shards(samples, plan, owner_table):
    windows = samples.shape[1] // HOP * lax.axis_size("tm")
    edge = lax.ppermute(samples[:, :HOP], "tm", [(1, 0), (2, 1), (3, 2)])
    own = whitened_spectra(samples, edge)
    slots = slot_table()
    v = basis_columns(windows, slots)
    slots = jnp.concatenate([slots, (lax.axis_index("tm") % 2).astype(jnp.int32)[None]])
    padded = np.zeros((104, RANK))
    padded[:LAGS] = lag_factors(windows)[0]
    high, low = split_bf16(padded)
    u = jnp.asarray(np.concatenate([high, low, high], axis=1))
    everyone = lax.all_to_all(own.reshape((32, 4) + own.shape[1:]), "chan", 0, 0)
    roots = owner_table[plan]
    parts = jnp.stack([lax.dynamic_index_in_dim(everyone, roots[s], 0, keepdims=False) for s in range(STEPS)])
    out = None
    for s, pieces in enumerate(gather_references(parts)):
        keep, send = lag_coefficients(own, pieces, slots, v)
        out = expand(s, u, *sum_over_spans(keep, send), out)
    return out.reshape(STEPS, LAGS, 32, 128).transpose(2, 0, 1, 3)


def solution(mesh):
    placed = (P("chan", "tm"), P(), P())
    return jax.shard_map(
        shards, mesh=mesh, in_specs=placed, out_specs=P("tm", None, None, "chan"), check_vma=False
    )
```

```python
import functools
import math

import jax
import jax.numpy as jnp
import ml_dtypes
import numpy as np
from jax import lax
from jax.experimental import pallas as pl
from jax.experimental.pallas import tpu as pltpu
from jax.sharding import PartitionSpec as P

WINLEN = 1024
HOP = 512
BINS = 128
BIN0 = 16
SMOOTH = 4
LAGS = 101
STEPS = 3
HALF_RANK = 24
RANK = 2 * HALF_RANK
GROUP = 8
magnitude_eps = 1e-06
water_level = 0.25
VMEM_BYTES = 60 * 1024 * 1024


def dft_table():
    n = np.arange(WINLEN)
    k = BIN0 + np.arange(BINS)
    angles = 2.0 * math.pi / WINLEN * (k[:, None] * n[None, :] % WINLEN)
    taper = 0.5 - 0.5 * np.cos(2.0 * math.pi / WINLEN * n)
    table = np.concatenate([np.cos(angles) * taper, -np.sin(angles) * taper], axis=0)
    return table.astype(np.float32).astype(ml_dtypes.bfloat16)


def band_tables():
    f = np.arange(BINS)
    inside = (np.abs(f[:, None] - f[None, :]) <= SMOOTH).astype(np.float32)
    counts = inside.sum(axis=1)
    return np.tile(inside, (1, 2)).astype(ml_dtypes.bfloat16), (1.0 / counts)[:, None].astype(np.float32)


def dot(a, b):
    return math.fsum(p * q for p, q in zip(a, b))


def row_basis(rows, count):
    left = [list(r) for r in rows]
    basis = []
    for _ in range(count):
        norms = [dot(r, r) for r in left]
        best = max(range(len(left)), key=lambda i: norms[i])
        q = left[best]
        for _ in range(2):
            for b in basis:
                d = dot(q, b)
                q = [x - d * y for x, y in zip(q, b)]
            size = math.sqrt(dot(q, q))
            q = [x / size for x in q]
        basis.append(q)
        for i, r in enumerate(left):
            d = dot(r, q)
            left[i] = [x - d * y for x, y in zip(r, q)]
    return basis


@functools.cache
def lag_factors(windows):
    factor = 1.0 / math.sqrt(BINS * windows)
    mid = LAGS // 2
    bins = range(BIN0, BIN0 + BINS)

    def angle(tau, k):
        return 2.0 * math.pi / WINLEN * (tau * k % WINLEN)

    even = [[math.cos(angle(t, k)) for k in bins] for t in range(mid + 1)]
    odd = [[-math.sin(angle(t, k)) for k in bins] for t in range(1, mid + 1)]
    even_basis = row_basis(even, HALF_RANK)
    odd_basis = row_basis(odd, HALF_RANK)
    even_u = np.array([[dot(r, b) for b in even_basis] for r in even])
    odd_u = np.array([[dot(r, b) for b in odd_basis] for r in odd])
    u = np.zeros((LAGS, RANK))
    for t in range(LAGS):
        tau = t - mid
        u[t, :HALF_RANK] = even_u[abs(tau)]
        if tau:
            u[t, HALF_RANK:] = math.copysign(1.0, tau) * odd_u[abs(tau) - 1]
    return u * factor, np.array(even_basis), np.array(odd_basis)


def split_bf16(value):
    high = value.astype(np.float32).astype(ml_dtypes.bfloat16)
    low = (value - high.astype(np.float64)).astype(np.float32).astype(ml_dtypes.bfloat16)
    return high, low


def bin_order():
    order = []
    for j in range(32):
        x, z, y = j // 8, j // 2 % 4, j % 2
        order += [2 * j, 2 * j + 1]
        order += [64 + 2 * ((z * 4 + x) * 2 + y), 65 + 2 * ((z * 4 + x) * 2 + y)]
    return np.array(order)


def spectra_kernel(chunk, x_ref, next_ref, edge_ref, table_ref, band_ref, inverse_ref, out_ref, rows):
    i = pl.program_id(0)
    tail = jnp.where(i == pl.num_programs(0) - 1, edge_ref[...], next_ref[...])
    pairs = range(chunk // 2)
    spectra, magnitudes, parts = [], [], []
    for pair in pairs:
        frames = []
        for w in (2 * pair, 2 * pair + 1):
            if w == chunk - 1:
                frames.append(jnp.concatenate([x_ref[:, w * HOP :], tail], axis=1))
            else:
                frames.append(x_ref[:, w * HOP : w * HOP + WINLEN])
        spectra.append(
            lax.dot_general(
                table_ref[...],
                jnp.concatenate(frames, axis=0),
                (((1,), (1,)), ((), ())),
                preferred_element_type=jnp.float32,
            )
        )
    for value in spectra:
        re, im = value[:BINS], value[BINS:]
        magnitude = jnp.sqrt(re * re + im * im + magnitude_eps)
        high = magnitude.astype(jnp.bfloat16)
        low = (magnitude - high.astype(jnp.float32)).astype(jnp.bfloat16)
        magnitudes.append(magnitude)
        parts.append(jnp.concatenate([high, low], axis=0))
    totals = [jnp.dot(band_ref[...], p, preferred_element_type=jnp.float32) for p in parts]
    for pair in pairs:
        mean = jnp.sum(magnitudes[pair], axis=0, keepdims=True) * (1.0 / BINS)
        scale = 1.0 / (totals[pair] * inverse_ref[...] + water_level * mean)
        for part in range(2):
            white = spectra[pair][part * BINS : (part + 1) * BINS] * scale
            for h in range(2):
                row = part * chunk + 2 * pair + h
                rows[pl.ds(row, BINS, stride=2 * chunk), :] = white[:, h * 128 : (h + 1) * 128]
    for q, f in enumerate(bin_order()):
        out_ref[q] = rows[2 * chunk * int(f) : 2 * chunk * (int(f) + 1), :].astype(jnp.bfloat16)


def whitened_spectra(samples, edge):
    channels, length = samples.shape
    windows = length // HOP
    band, inverse = band_tables()
    whole = lambda shape: pl.BlockSpec(shape, lambda i: (0,) * len(shape))
    return pl.pallas_call(
        functools.partial(spectra_kernel, GROUP),
        grid=(windows // GROUP,),
        out_shape=jax.ShapeDtypeStruct((BINS, 2 * windows, channels), jnp.bfloat16),
        in_specs=[
            pl.BlockSpec((channels, GROUP * HOP), lambda i: (0, i)),
            pl.BlockSpec((channels, HOP), lambda i: (0, jnp.minimum((i + 1) * GROUP, windows - 1))),
            whole((channels, HOP)),
            whole((2 * BINS, WINLEN)),
            whole((BINS, 2 * BINS)),
            whole((BINS, 1)),
        ],
        out_specs=pl.BlockSpec((BINS, 2 * GROUP, channels), lambda i: (0, i, 0)),
        scratch_shapes=[pltpu.VMEM((BINS * 2 * GROUP, channels), jnp.float32)],
        compiler_params=pltpu.CompilerParams(vmem_limit_bytes=VMEM_BYTES),
        name="spectra",
    )(samples, samples, edge, jnp.asarray(dft_table()), jnp.asarray(band), jnp.asarray(inverse))


def add_cross(spans, pieces, slots, base, row, real_rows, imag_rows):
    results = []
    for piece, size in pieces:
        for j in range(size):
            slot = slots[base + len(results)]
            width = piece.shape[3] // len(spans)
            total = None
            for n, span in enumerate(spans):
                own = span[slot]
                turned = []
                for r in range(0, own.shape[0], 2 * GROUP):
                    turned += [own[r + GROUP : r + 2 * GROUP], -own[r : r + GROUP]]
                cross = lax.dot_general(
                    piece[0, j][:, n * width : (n + 1) * width],
                    jnp.concatenate([own, jnp.concatenate(turned, axis=0)], axis=1),
                    (((0,), (0,)), ((), ())),
                    preferred_element_type=jnp.float32,
                )
                total = cross if total is None else total + cross
            results.append(total)
    for j, cross in enumerate(results):
        real_rows[pl.ds(base + j, cross.shape[0], stride=row), :] = cross[:, :128]
        imag_rows[pl.ds(base + j, cross.shape[0], stride=row), :] = cross[:, 128:]


def coefficients(v_ref, real_rows, imag_rows, row, bins, channels):
    results = []
    for n in range(0, len(channels), 2):
        halves = []
        for b in channels[n : n + 2]:
            start = pl.multiple_of(b * row, 8)
            halves.append(
                jnp.concatenate(
                    [real_rows[pl.ds(start, bins), :], imag_rows[pl.ds(start, bins), :]], axis=0
                ).astype(jnp.bfloat16)
            )
        results.append(jnp.dot(v_ref[...], jnp.concatenate(halves, axis=1), preferred_element_type=jnp.float32))
    totals = []
    for both in results:
        total = both[:RANK] + both[RANK:]
        totals += [total[:, :128], total[:, 128:]]
    return totals


def near_kernel(count, slots_ref, v_ref, own_ref, next_ref, *refs):
    pieces, (out_ref, real_rows, imag_rows) = refs[:count], refs[count:]
    size = pieces[0].shape[1]
    bins = count * size
    row = bins + 8
    for n in range(0, count, 2):
        chosen = [(p, size) for p in pieces[n : n + 2]]
        add_cross((own_ref, next_ref), chosen, slots_ref, n * size, row, real_rows, imag_rows)

    def some(n, carry):
        channels = [n * 32 + j for j in range(32)]
        totals = coefficients(v_ref, real_rows, imag_rows, row, bins, channels)
        for b, total in zip(channels, totals):
            out_ref[0, b] = total
        return carry

    lax.fori_loop(0, 2, some, 0)


def far_kernel(step, count, slots_ref, v_ref, own_hbm, next_hbm, near_hbm, *refs):
    pieces = refs[:count]
    keep_ref, send_ref, own_ref, next_ref, near_ref, other_ref, real_rows, imag_rows, own_sems, near_sem, sems = refs[
        count:
    ]
    size = pieces[0].shape[1]
    bins = count * size
    row = bins + 8
    copies = [
        pltpu.make_async_copy(p.at[step], other_ref.at[0, pl.ds(size * i, size)], sems.at[i])
        for i, p in enumerate(pieces)
    ]
    for n, (source, target) in enumerate(((own_hbm, own_ref), (next_hbm, next_ref))):
        copies += [
            pltpu.make_async_copy(source.at[slots_ref[j]], target.at[j], own_sems.at[n * bins + j])
            for j in range(bins)
        ]
    near_copy = pltpu.make_async_copy(near_hbm.at[step], near_ref, near_sem)
    for copy in copies + [near_copy]:
        copy.start()
    for copy in copies:
        copy.wait()
    add_cross((own_ref, next_ref), [(other_ref, bins)], range(bins), 0, row, real_rows, imag_rows)
    near_copy.wait()
    core = slots_ref[bins]
    for out_ref, which in ((send_ref, 1 - core), (keep_ref, core)):
        channels = [which * 32 + j for j in range(32)]
        totals = coefficients(v_ref, real_rows, imag_rows, row, bins, channels)
        for j, total in enumerate(totals):
            out_ref[j] = (near_ref[channels[j]] + total).astype(out_ref.dtype)


def step_block(shape):
    return pl.BlockSpec((1,) + shape, lambda s: (s,) + (0,) * len(shape))


def near_coefficients(own, across, pieces, slots, v):
    bins = sum(p.shape[1] for p in pieces)
    whole = lambda a: pl.BlockSpec(a.shape, lambda s: (0,) * a.ndim)
    return pl.pallas_call(
        functools.partial(near_kernel, len(pieces)),
        grid=(STEPS,),
        out_shape=jax.ShapeDtypeStruct((STEPS, 64, RANK, 128), jnp.float32),
        in_specs=[pl.BlockSpec(memory_space=pltpu.SMEM), whole(v), whole(own), whole(across)]
        + [step_block(p.shape[1:]) for p in pieces],
        out_specs=step_block((64, RANK, 128)),
        scratch_shapes=[pltpu.VMEM((64 * (bins + 8), 128), jnp.float32)] * 2,
        compiler_params=pltpu.CompilerParams(vmem_limit_bytes=VMEM_BYTES),
        name="near",
    )(slots, v, own, across, *pieces)


def all_coefficients(step, own, across, near, pieces, slots, v):
    vmem = pl.BlockSpec(memory_space=pltpu.VMEM)
    hbm = pl.BlockSpec(memory_space=pl.ANY)
    bins = sum(p.shape[1] for p in pieces)
    rows = (32, RANK, 128)
    return pl.pallas_call(
        functools.partial(far_kernel, step, len(pieces)),
        out_shape=[jax.ShapeDtypeStruct(rows, jnp.float32), jax.ShapeDtypeStruct(rows, jnp.bfloat16)],
        in_specs=[pl.BlockSpec(memory_space=pltpu.SMEM), vmem] + [hbm] * (3 + len(pieces)),
        out_specs=[vmem, vmem],
        scratch_shapes=[
            pltpu.VMEM((bins,) + own.shape[1:], jnp.bfloat16),
            pltpu.VMEM((bins,) + own.shape[1:], jnp.bfloat16),
            pltpu.VMEM(near.shape[1:], jnp.float32),
            pltpu.VMEM((1, bins) + own.shape[1:], jnp.bfloat16),
        ]
        + [pltpu.VMEM((64 * (bins + 8), 128), jnp.float32)] * 2
        + [
            pltpu.SemaphoreType.DMA((2 * bins,)),
            pltpu.SemaphoreType.DMA,
            pltpu.SemaphoreType.DMA((len(pieces),)),
        ],
        compiler_params=pltpu.CompilerParams(vmem_limit_bytes=VMEM_BYTES),
        name="far",
    )(slots, v, own, across, near, *pieces)


def expand_kernel(step, u_ref, keep_ref, got_ref, *refs):
    out_ref, lags_ref, sem = refs[-3:]
    count = keep_ref.shape[0]
    results = []
    for n in range(0, count, 2):
        value = jnp.concatenate([keep_ref[b] + got_ref[b].astype(jnp.float32) for b in (n, n + 1)], axis=1)
        high = value.astype(jnp.bfloat16)
        low = (value - high.astype(jnp.float32)).astype(jnp.bfloat16)
        results.append(
            jnp.dot(u_ref[...], jnp.concatenate([high, high, low], axis=0), preferred_element_type=jnp.float32)
        )
    for n, lags in enumerate(results):
        lags_ref[pl.ds(2 * n, LAGS, stride=count), :] = lags[:LAGS, :128]
        lags_ref[pl.ds(2 * n + 1, LAGS, stride=count), :] = lags[:LAGS, 128:]
    copy = pltpu.make_async_copy(lags_ref, out_ref.at[step], sem)
    copy.start()
    copy.wait()


def expand(step, u, keep, got, before):
    vmem = pl.BlockSpec(memory_space=pltpu.VMEM)
    hbm = pl.BlockSpec(memory_space=pl.ANY)
    shape = (LAGS * keep.shape[0], 128)
    held = [] if before is None else [before]
    return pl.pallas_call(
        functools.partial(expand_kernel, step),
        out_shape=jax.ShapeDtypeStruct((STEPS,) + shape, jnp.float32),
        in_specs=[vmem] * 3 + [hbm] * len(held),
        out_specs=hbm,
        scratch_shapes=[pltpu.VMEM(shape, jnp.float32), pltpu.SemaphoreType.DMA],
        input_output_aliases={3: 0} if held else {},
        compiler_params=pltpu.CompilerParams(vmem_limit_bytes=VMEM_BYTES),
        name="expand",
    )(u, keep, got, *held)


def place(x, z, y):
    return (x % 4) * 8 + (z % 4) * 2 + y % 2


def shift(value, dx=0, dz=0, dy=0):
    pairs = [(place(x, z, y), place(x + dx, z + dz, y + dy)) for x in range(4) for z in range(4) for y in range(2)]
    return lax.ppermute(value, "chan", pairs)


def around(value, axis):
    return [value] + [shift(value, **{axis: step}) for step in (1, -1, 2)]


def gather_references(parts):
    other = shift(parts, dy=1)
    first = jnp.concatenate([parts[:, :2], other[:, :2]], axis=1)
    second = jnp.concatenate([parts[:, 2:], other[:, 2:]], axis=1)
    plane_a = jnp.concatenate(around(first, "dz"), axis=1)
    plane_b = jnp.concatenate(around(second, "dx"), axis=1)
    return plane_a, plane_b


def plane_slots(last):
    me = lax.axis_index("chan")
    x, z, y = me // 8, me // 2 % 4, me % 2
    plane, dy, e = np.meshgrid(np.array((0, -1, 1, 2)), np.arange(2), np.arange(2), indexing="ij")
    plane, dy, e = (t.reshape(-1).astype(np.int32) for t in (plane, dy, e))
    y_of = (y + dy) % 2
    first = (((x + last + 4) % 4) * 8 + ((z + plane + 4) % 4) * 2 + y_of) * 4 + e
    second = (((x + plane + 4) % 4) * 8 + ((z + last + 4) % 4) * 2 + y_of) * 4 + 2 + e
    return [first, second]


def from_other_core(value):
    return lax.ppermute(value, "tm", [(0, 1), (1, 0), (2, 3), (3, 2)])


def from_other_chip(value):
    return lax.ppermute(value, "tm", [(0, 2), (2, 0), (1, 3), (3, 1)])


def windows_of_both_chips(parts):
    got = from_other_chip(parts)
    lower = lax.axis_index("tm") < 2
    middle = parts.shape[-1] // 2
    own = jnp.where(lower, parts, jnp.roll(parts, middle, axis=-1))
    other = jnp.where(lower, jnp.roll(got, middle, axis=-1), got)
    return jnp.where(jnp.arange(parts.shape[-1]) < middle, own, other)


def basis_columns(windows, slots):
    _, even, odd = lag_factors(windows)
    parts = [split_bf16(t[:, bin_order()]) for t in (even, odd)]
    table = np.concatenate([parts[0][0], parts[1][0], parts[0][1], parts[1][1]], axis=0)
    chosen = (jnp.arange(BINS, dtype=jnp.int32)[:, None] == slots[None, :]).astype(jnp.bfloat16)
    table = jnp.dot(jnp.asarray(table), chosen, preferred_element_type=jnp.float32).astype(jnp.bfloat16)
    is_odd = (np.arange(2 * RANK) // HALF_RANK % 2 == 1)[:, None]
    nothing = jnp.zeros_like(table)
    real, imag = jnp.where(is_odd, nothing, table), jnp.where(is_odd, table, nothing)
    return lambda start, stop: jnp.concatenate([real[:, start:stop], imag[:, start:stop]], axis=1)


def shards(samples, plan, owner_table):
    windows = samples.shape[1] // HOP * lax.axis_size("tm")
    edge = lax.ppermute(samples[:, :HOP], "tm", [(1, 0), (2, 1), (3, 2)])
    own = whitened_spectra(samples, edge)
    slots = jnp.concatenate(sum([plane_slots(last) for last in (0, -1, 1, 2)], [])).astype(jnp.int32)
    v = basis_columns(windows, slots)
    core = (lax.axis_index("tm") % 2).astype(jnp.int32)[None]
    near_bins = BINS * 3 // 4
    padded = np.zeros((104, RANK))
    padded[:LAGS] = lag_factors(windows)[0]
    high, low = split_bf16(padded)
    u = jnp.asarray(np.concatenate([high, low, high], axis=1))
    tables = (slots[:near_bins], jnp.concatenate([slots[near_bins:], core]), v(0, near_bins), v(near_bins, BINS))
    everyone = lax.all_to_all(own.reshape((32, 4) + own.shape[1:]), "chan", 0, 0)
    everyone, tables = lax.optimization_barrier((everyone, tables))
    near_slots, far_slots, near_v, far_v = tables
    roots = owner_table[plan]
    parts = jnp.stack([lax.dynamic_index_in_dim(everyone, roots[s], 0, keepdims=False) for s in range(STEPS)])
    parts, own = lax.optimization_barrier((parts, own))
    across = from_other_chip(own)
    plane_a, plane_b = gather_references(windows_of_both_chips(parts))
    near = [
        shift(plane_a, dx=1),
        shift(plane_b, dz=1),
        shift(plane_a, dx=-1),
        shift(plane_b, dz=-1),
    ]
    near = lax.optimization_barrier(near)
    half = plane_a.shape[1] // 2
    far = [
        shift(near[0][:, :half], dx=1),
        shift(near[2][:, half:], dx=-1),
        shift(near[1][:, :half], dz=1),
        shift(near[3][:, half:], dz=-1),
    ]
    partial = near_coefficients(own, across, [plane_a, plane_b] + near, near_slots, near_v)
    far, partial = lax.optimization_barrier((far, partial))
    keep, got = [None] * STEPS, [None] * STEPS
    for s in range(STEPS):
        keep[s], send = all_coefficients(s, own, across, partial, far, far_slots, far_v)
        got[s] = from_other_core(send)
        if s + 1 < STEPS:
            partial, _ = lax.optimization_barrier((partial, send))
    out = None
    for s in range(STEPS):
        out = expand(s, u, keep[s], got[s], out)
    return out.reshape(STEPS, LAGS, 32, 128).transpose(2, 0, 1, 3)


def solution(mesh):
    placed = (P("chan", "tm"), P(), P())
    return jax.shard_map(
        shards, mesh=mesh, in_specs=placed, out_specs=P("tm", None, None, "chan"), check_vma=False
    )
```

```python
import functools
import math

import jax
import jax.numpy as jnp
import ml_dtypes
import numpy as np
from jax import lax
from jax.experimental import pallas as pl
from jax.experimental.pallas import tpu as pltpu
from jax.sharding import PartitionSpec as P

WINLEN = 1024
HOP = 512
BINS = 128
BIN0 = 16
SMOOTH = 4
LAGS = 101
STEPS = 3
HALF_RANK = 24
RANK = 2 * HALF_RANK
GROUP = 8
magnitude_eps = 1e-06
water_level = 0.25
VMEM_BYTES = 60 * 1024 * 1024


def dft_table():
    n = np.arange(WINLEN)
    k = BIN0 + np.arange(BINS)
    angles = 2.0 * math.pi / WINLEN * (k[:, None] * n[None, :] % WINLEN)
    taper = 0.5 - 0.5 * np.cos(2.0 * math.pi / WINLEN * n)
    table = np.concatenate([np.cos(angles) * taper, -np.sin(angles) * taper], axis=0)
    return table.astype(np.float32).astype(ml_dtypes.bfloat16)


def band_tables():
    f = np.arange(BINS)
    inside = (np.abs(f[:, None] - f[None, :]) <= SMOOTH).astype(np.float32)
    counts = inside.sum(axis=1)
    return np.tile(inside, (1, 2)).astype(ml_dtypes.bfloat16), (1.0 / counts)[:, None].astype(np.float32)


def dot(a, b):
    return math.fsum(p * q for p, q in zip(a, b))


def row_basis(rows, count):
    left = [list(r) for r in rows]
    basis = []
    for _ in range(count):
        norms = [dot(r, r) for r in left]
        best = max(range(len(left)), key=lambda i: norms[i])
        q = left[best]
        for _ in range(2):
            for b in basis:
                d = dot(q, b)
                q = [x - d * y for x, y in zip(q, b)]
            size = math.sqrt(dot(q, q))
            q = [x / size for x in q]
        basis.append(q)
        for i, r in enumerate(left):
            d = dot(r, q)
            left[i] = [x - d * y for x, y in zip(r, q)]
    return basis


@functools.cache
def lag_factors(windows):
    factor = 1.0 / math.sqrt(BINS * windows)
    mid = LAGS // 2
    bins = range(BIN0, BIN0 + BINS)

    def angle(tau, k):
        return 2.0 * math.pi / WINLEN * (tau * k % WINLEN)

    even = [[math.cos(angle(t, k)) for k in bins] for t in range(mid + 1)]
    odd = [[-math.sin(angle(t, k)) for k in bins] for t in range(1, mid + 1)]
    even_basis = row_basis(even, HALF_RANK)
    odd_basis = row_basis(odd, HALF_RANK)
    even_u = np.array([[dot(r, b) for b in even_basis] for r in even])
    odd_u = np.array([[dot(r, b) for b in odd_basis] for r in odd])
    u = np.zeros((LAGS, RANK))
    for t in range(LAGS):
        tau = t - mid
        u[t, :HALF_RANK] = even_u[abs(tau)]
        if tau:
            u[t, HALF_RANK:] = math.copysign(1.0, tau) * odd_u[abs(tau) - 1]
    return u * factor, np.array(even_basis), np.array(odd_basis)


def split_bf16(value):
    high = value.astype(np.float32).astype(ml_dtypes.bfloat16)
    low = (value - high.astype(np.float64)).astype(np.float32).astype(ml_dtypes.bfloat16)
    return high, low


def bin_order():
    order = []
    for j in range(32):
        x, z, y = j // 8, j // 2 % 4, j % 2
        order += [2 * j, 2 * j + 1]
        order += [64 + 2 * ((z * 4 + x) * 2 + y), 65 + 2 * ((z * 4 + x) * 2 + y)]
    return np.array(order)


def spectra_kernel(chunk, x_ref, next_ref, edge_ref, table_ref, band_ref, inverse_ref, out_ref, rows):
    i = pl.program_id(0)
    tail = jnp.where(i == pl.num_programs(0) - 1, edge_ref[...], next_ref[...])
    pairs = range(chunk // 2)
    spectra, magnitudes, parts = [], [], []
    for pair in pairs:
        frames = []
        for w in (2 * pair, 2 * pair + 1):
            if w == chunk - 1:
                frames.append(jnp.concatenate([x_ref[:, w * HOP :], tail], axis=1))
            else:
                frames.append(x_ref[:, w * HOP : w * HOP + WINLEN])
        spectra.append(
            lax.dot_general(
                table_ref[...],
                jnp.concatenate(frames, axis=0),
                (((1,), (1,)), ((), ())),
                preferred_element_type=jnp.float32,
            )
        )
    for value in spectra:
        re, im = value[:BINS], value[BINS:]
        magnitude = jnp.sqrt(re * re + im * im + magnitude_eps)
        high = magnitude.astype(jnp.bfloat16)
        low = (magnitude - high.astype(jnp.float32)).astype(jnp.bfloat16)
        magnitudes.append(magnitude)
        parts.append(jnp.concatenate([high, low], axis=0))
    totals = [jnp.dot(band_ref[...], p, preferred_element_type=jnp.float32) for p in parts]
    for pair in pairs:
        mean = jnp.sum(magnitudes[pair], axis=0, keepdims=True) * (1.0 / BINS)
        scale = 1.0 / (totals[pair] * inverse_ref[...] + water_level * mean)
        for part in range(2):
            white = spectra[pair][part * BINS : (part + 1) * BINS] * scale
            for h in range(2):
                row = part * chunk + 2 * pair + h
                rows[pl.ds(row, BINS, stride=2 * chunk), :] = white[:, h * 128 : (h + 1) * 128]
    for q, f in enumerate(bin_order()):
        out_ref[q] = rows[2 * chunk * int(f) : 2 * chunk * (int(f) + 1), :].astype(jnp.bfloat16)


def whitened_spectra(samples, edge):
    channels, length = samples.shape
    windows = length // HOP
    band, inverse = band_tables()
    whole = lambda shape: pl.BlockSpec(shape, lambda i: (0,) * len(shape))
    return pl.pallas_call(
        functools.partial(spectra_kernel, GROUP),
        grid=(windows // GROUP,),
        out_shape=jax.ShapeDtypeStruct((BINS, 2 * windows, channels), jnp.bfloat16),
        in_specs=[
            pl.BlockSpec((channels, GROUP * HOP), lambda i: (0, i)),
            pl.BlockSpec((channels, HOP), lambda i: (0, jnp.minimum((i + 1) * GROUP, windows - 1))),
            whole((channels, HOP)),
            whole((2 * BINS, WINLEN)),
            whole((BINS, 2 * BINS)),
            whole((BINS, 1)),
        ],
        out_specs=pl.BlockSpec((BINS, 2 * GROUP, channels), lambda i: (0, i, 0)),
        scratch_shapes=[pltpu.VMEM((BINS * 2 * GROUP, channels), jnp.float32)],
        compiler_params=pltpu.CompilerParams(vmem_limit_bytes=VMEM_BYTES),
        name="spectra",
    )(samples, samples, edge, jnp.asarray(dft_table()), jnp.asarray(band), jnp.asarray(inverse))


def add_cross(spans, pieces, slots, base, row, real_rows, imag_rows):
    results = []
    for piece, size in pieces:
        for j in range(size):
            slot = slots[base + len(results)]
            width = piece.shape[-1] // len(spans)
            total = None
            for n, span in enumerate(spans):
                own = span(slot)
                turned = []
                for r in range(0, own.shape[0], 2 * GROUP):
                    turned += [own[r + GROUP : r + 2 * GROUP], -own[r : r + GROUP]]
                cross = lax.dot_general(
                    piece[0, j][:, n * width : (n + 1) * width],
                    jnp.concatenate([own, jnp.concatenate(turned, axis=0)], axis=1),
                    (((0,), (0,)), ((), ())),
                    preferred_element_type=jnp.float32,
                )
                total = cross if total is None else total + cross
            results.append(total)
    for j, cross in enumerate(results):
        real_rows[pl.ds(base + j, cross.shape[0], stride=row), :] = cross[:, :128]
        imag_rows[pl.ds(base + j, cross.shape[0], stride=row), :] = cross[:, 128:]


def coefficients(v_ref, real_rows, imag_rows, row, bins, channels):
    results = []
    for n in range(0, len(channels), 2):
        halves = []
        for b in channels[n : n + 2]:
            start = pl.multiple_of(b * row, 8)
            halves.append(
                jnp.concatenate(
                    [real_rows[pl.ds(start, bins), :], imag_rows[pl.ds(start, bins), :]], axis=0
                ).astype(jnp.bfloat16)
            )
        results.append(jnp.dot(v_ref[...], jnp.concatenate(halves, axis=1), preferred_element_type=jnp.float32))
    totals = []
    for both in results:
        total = both[:RANK] + both[RANK:]
        totals += [total[:, :128], total[:, 128:]]
    return totals


def both_spans(own_ref, across_refs):
    middle = own_ref.shape[1] // 2
    return [
        lambda slot, start=start, across=across: jnp.concatenate(
            [own_ref[slot, start : start + middle], across[slot]], axis=0
        )
        for start, across in zip((0, middle), across_refs)
    ]


def halves_of(planes):
    return [(plane.at[half], plane.shape[2]) for plane in planes for half in range(2)]


def near_kernel(count, slots_ref, v_ref, own_ref, upper_ref, lower_ref, *refs):
    pieces, (out_ref, real_rows, imag_rows) = refs[:count], refs[count:]
    spans = both_spans(own_ref, (upper_ref, lower_ref))
    size = pieces[0].shape[2]
    bins = 2 * count * size
    row = bins + 8
    for n in range(0, count, 2):
        add_cross(spans, halves_of(pieces[n : n + 2]), slots_ref, 2 * n * size, row, real_rows, imag_rows)

    def some(n, carry):
        channels = [n * 32 + j for j in range(32)]
        totals = coefficients(v_ref, real_rows, imag_rows, row, bins, channels)
        for b, total in zip(channels, totals):
            out_ref[0, b] = total
        return carry

    lax.fori_loop(0, 2, some, 0)


def far_kernel(count, slots_ref, v_ref, own_hbm, upper_hbm, lower_hbm, near_ref, *refs):
    pieces, refs = refs[:count], refs[count:]
    keep_ref, send_ref, own_ref, upper_ref, lower_ref, real_rows, imag_rows, sems = refs
    size = pieces[0].shape[1]
    bins = count * size
    row = bins + 8

    @pl.when(pl.program_id(0) == 0)
    def _():
        copies = []
        for n, (source, target) in enumerate(((own_hbm, own_ref), (upper_hbm, upper_ref), (lower_hbm, lower_ref))):
            copies += [
                pltpu.make_async_copy(source.at[slots_ref[j]], target.at[j], sems.at[n * bins + j])
                for j in range(bins)
            ]
        for copy in copies:
            copy.start()
        for copy in copies:
            copy.wait()

    spans = both_spans(own_ref, (upper_ref, lower_ref))
    add_cross(spans, [(p, size) for p in pieces], range(bins), 0, row, real_rows, imag_rows)
    core = slots_ref[bins]
    for out_ref, which in ((send_ref, 1 - core), (keep_ref, core)):
        channels = [which * 32 + j for j in range(32)]
        totals = coefficients(v_ref, real_rows, imag_rows, row, bins, channels)
        for j, total in enumerate(totals):
            out_ref[0, j] = (near_ref[0, channels[j]] + total).astype(out_ref.dtype)


def step_block(shape):
    return pl.BlockSpec((1,) + shape, lambda s: (s,) + (0,) * len(shape))


def near_coefficients(own, across, pieces, slots, v):
    bins = sum(p.shape[0] * p.shape[2] for p in pieces)
    whole = lambda a: pl.BlockSpec(a.shape, lambda s: (0,) * a.ndim)
    return pl.pallas_call(
        functools.partial(near_kernel, len(pieces)),
        grid=(STEPS,),
        out_shape=jax.ShapeDtypeStruct((STEPS, 64, RANK, 128), jnp.float32),
        in_specs=[pl.BlockSpec(memory_space=pltpu.SMEM), whole(v), whole(own)]
        + [whole(a) for a in across]
        + [pl.BlockSpec((2, 1) + p.shape[2:], lambda s: (0, s, 0, 0, 0)) for p in pieces],
        out_specs=step_block((64, RANK, 128)),
        scratch_shapes=[pltpu.VMEM((64 * (bins + 8), 128), jnp.float32)] * 2,
        compiler_params=pltpu.CompilerParams(vmem_limit_bytes=VMEM_BYTES),
        name="near",
    )(slots, v, own, *across, *pieces)


def all_coefficients(own, across, near, pieces, slots, v):
    hbm = pl.BlockSpec(memory_space=pl.ANY)
    bins = sum(p.shape[1] for p in pieces)
    rows = (32, RANK, 128)
    return pl.pallas_call(
        functools.partial(far_kernel, len(pieces)),
        grid=(STEPS,),
        out_shape=[
            jax.ShapeDtypeStruct((STEPS,) + rows, jnp.float32),
            jax.ShapeDtypeStruct((STEPS,) + rows, jnp.bfloat16),
        ],
        in_specs=[pl.BlockSpec(memory_space=pltpu.SMEM), pl.BlockSpec(v.shape, lambda s: (0, 0))]
        + [hbm] * 3
        + [step_block(a.shape[1:]) for a in [near] + pieces],
        out_specs=[step_block(rows)] * 2,
        scratch_shapes=[pltpu.VMEM((bins,) + a.shape[1:], jnp.bfloat16) for a in (own,) + across]
        + [pltpu.VMEM((64 * (bins + 8), 128), jnp.float32)] * 2
        + [pltpu.SemaphoreType.DMA((3 * bins,))],
        compiler_params=pltpu.CompilerParams(vmem_limit_bytes=VMEM_BYTES),
        name="far",
    )(slots, v, own, *across, near, *pieces)


def expand_kernel(u_ref, keep_ref, got_ref, out_ref):
    count = keep_ref.shape[1]
    results = []
    for n in range(0, count, 2):
        value = jnp.concatenate([keep_ref[0, b] + got_ref[0, b].astype(jnp.float32) for b in (n, n + 1)], axis=1)
        high = value.astype(jnp.bfloat16)
        low = (value - high.astype(jnp.float32)).astype(jnp.bfloat16)
        results.append(
            jnp.dot(u_ref[...], jnp.concatenate([high, high, low], axis=0), preferred_element_type=jnp.float32)
        )
    for n, lags in enumerate(results):
        out_ref[0, pl.ds(2 * n, LAGS, stride=count), :] = lags[:LAGS, :128]
        out_ref[0, pl.ds(2 * n + 1, LAGS, stride=count), :] = lags[:LAGS, 128:]


def expand(u, keep, got):
    shape = (LAGS * keep.shape[1], 128)
    return pl.pallas_call(
        expand_kernel,
        grid=(STEPS,),
        out_shape=jax.ShapeDtypeStruct((STEPS,) + shape, jnp.float32),
        in_specs=[pl.BlockSpec(u.shape, lambda s: (0, 0)), step_block(keep.shape[1:]), step_block(got.shape[1:])],
        out_specs=step_block(shape),
        compiler_params=pltpu.CompilerParams(vmem_limit_bytes=VMEM_BYTES),
        name="expand",
    )(u, keep, got)


def place(x, z, y):
    return (x % 4) * 8 + (z % 4) * 2 + y % 2


def shift(value, dx=0, dz=0, dy=0):
    pairs = [(place(x, z, y), place(x + dx, z + dz, y + dy)) for x in range(4) for z in range(4) for y in range(2)]
    return lax.ppermute(value, "chan", pairs)


def plane(own, axis):
    ahead, behind, far = [shift(own, **{axis: step}) for step in (1, -1, 2)]
    return jnp.stack([jnp.concatenate([own, ahead], axis=1), jnp.concatenate([behind, far], axis=1)])


def gather_planes(parts):
    pairs = [(4 * c + t, 4 * (c ^ 1) + (t ^ 2)) for c in range(32) for t in range(4)]
    middle, columns = parts.shape[2] // 2, parts.shape[3] // 2
    lower = lax.axis_index("tm") < 2
    sides = parts[..., :columns], parts[..., columns:]

    def packed(side):
        return jnp.concatenate([side[:, :, :middle], side[:, :, middle:]], axis=3)

    mine = packed(jnp.where(lower, sides[0], sides[1]))
    theirs = packed(jnp.where(lower, sides[1], sides[0]))
    beside = shift(mine, dy=1)
    beyond = from_other_chip(theirs)
    across = lax.ppermute(theirs, ("chan", "tm"), pairs)
    own = jnp.concatenate([mine, beyond], axis=2)
    other = jnp.concatenate([beside, across], axis=2)
    first = jnp.concatenate([own[:, :2], other[:, :2]], axis=1)
    second = jnp.concatenate([own[:, 2:], other[:, 2:]], axis=1)
    return lax.optimization_barrier((first, second))


def plane_slots(last):
    me = lax.axis_index("chan")
    x, z, y = me // 8, me // 2 % 4, me % 2
    plane, dy, e = np.meshgrid(np.array((0, -1, 1, 2)), np.arange(2), np.arange(2), indexing="ij")
    plane, dy, e = (t.reshape(-1).astype(np.int32) for t in (plane, dy, e))
    y_of = (y + dy) % 2
    first = (((x + last + 4) % 4) * 8 + ((z + plane + 4) % 4) * 2 + y_of) * 4 + e
    second = (((x + plane + 4) % 4) * 8 + ((z + last + 4) % 4) * 2 + y_of) * 4 + 2 + e
    return [first, second]


def from_other_core(value):
    return lax.ppermute(value, "tm", [(0, 1), (1, 0), (2, 3), (3, 2)])


def from_other_chip(value):
    return lax.ppermute(value, "tm", [(0, 2), (2, 0), (1, 3), (3, 1)])


def basis_columns(windows, slots):
    _, even, odd = lag_factors(windows)
    parts = [split_bf16(t[:, bin_order()]) for t in (even, odd)]
    table = np.concatenate([parts[0][0], parts[1][0], parts[0][1], parts[1][1]], axis=0)
    chosen = (jnp.arange(BINS, dtype=jnp.int32)[:, None] == slots[None, :]).astype(jnp.bfloat16)
    table = jnp.dot(jnp.asarray(table), chosen, preferred_element_type=jnp.float32).astype(jnp.bfloat16)
    is_odd = (np.arange(2 * RANK) // HALF_RANK % 2 == 1)[:, None]
    nothing = jnp.zeros_like(table)
    real, imag = jnp.where(is_odd, nothing, table), jnp.where(is_odd, table, nothing)
    return lambda start, stop: jnp.concatenate([real[:, start:stop], imag[:, start:stop]], axis=1)


def shards(samples, plan, owner_table):
    windows = samples.shape[1] // HOP * lax.axis_size("tm")
    edge = lax.ppermute(samples[:, :HOP], "tm", [(1, 0), (2, 1), (3, 2)])
    own = whitened_spectra(samples, edge)
    slots = jnp.concatenate(sum([plane_slots(last) for last in (0, -1, 1, 2)], [])).astype(jnp.int32)
    v = basis_columns(windows, slots)
    core = (lax.axis_index("tm") % 2).astype(jnp.int32)[None]
    near_bins = BINS * 3 // 4
    padded = np.zeros((104, RANK))
    padded[:LAGS] = lag_factors(windows)[0]
    high, low = split_bf16(padded)
    u = jnp.asarray(np.concatenate([high, low, high], axis=1))
    tables = (slots[:near_bins], jnp.concatenate([slots[near_bins:], core]), v(0, near_bins), v(near_bins, BINS))
    everyone = lax.all_to_all(own.reshape((32, 4) + own.shape[1:]), "chan", 0, 0)
    middle = own.shape[1] // 2
    leaving = own[:, :middle], own[:, middle:]
    everyone, tables, leaving = lax.optimization_barrier((everyone, tables, leaving))
    upper = from_other_chip(leaving[0])
    near_slots, far_slots, near_v, far_v = tables
    roots = owner_table[plan]
    parts = jnp.stack([lax.dynamic_index_in_dim(everyone, roots[s], 0, keepdims=False) for s in range(STEPS)])
    first, second = gather_planes(parts)
    plane_a, plane_b = plane(first, "dz"), plane(second, "dx")
    plane_a, plane_b, upper, lower = lax.optimization_barrier((plane_a, plane_b, upper, leaving[1]))
    across = upper, from_other_chip(lower)
    near = [
        shift(plane_a, dx=1),
        shift(plane_b, dz=1),
        shift(plane_a, dx=-1),
        shift(plane_b, dz=-1),
    ]
    far = [
        shift(near[0][0], dx=1),
        shift(near[2][1], dx=-1),
        shift(near[1][0], dz=1),
        shift(near[3][1], dz=-1),
    ]
    partial = near_coefficients(own, across, [plane_a, plane_b] + near, near_slots, near_v)
    far, partial = lax.optimization_barrier((far, partial))
    keep, send = all_coefficients(own, across, partial, far, far_slots, far_v)
    out = expand(u, keep, from_other_core(send))
    return out.reshape(STEPS, LAGS, 32, 128).transpose(2, 0, 1, 3)


def solution(mesh):
    placed = (P("chan", "tm"), P(), P())
    return jax.shard_map(
        shards, mesh=mesh, in_specs=placed, out_specs=P("tm", None, None, "chan"), check_vma=False
    )
```

```python
import functools
import math

import jax
import jax.numpy as jnp
import ml_dtypes
import numpy as np
from jax import lax
from jax.experimental import pallas as pl
from jax.experimental.pallas import tpu as pltpu
from jax.sharding import PartitionSpec as P

WINLEN = 1024
HOP = 512
BINS = 128
BIN0 = 16
SMOOTH = 4
LAGS = 101
STEPS = 3
HALF_RANK = 24
RANK = 2 * HALF_RANK
GROUP = 8
magnitude_eps = 1e-06
water_level = 0.25
VMEM_BYTES = 60 * 1024 * 1024


def dft_table():
    n = np.arange(WINLEN)
    k = BIN0 + np.arange(BINS)
    angles = 2.0 * math.pi / WINLEN * (k[:, None] * n[None, :] % WINLEN)
    taper = 0.5 - 0.5 * np.cos(2.0 * math.pi / WINLEN * n)
    table = np.concatenate([np.cos(angles) * taper, -np.sin(angles) * taper], axis=0)
    return table.astype(np.float32).astype(ml_dtypes.bfloat16)


def band_tables():
    f = np.arange(BINS)
    inside = (np.abs(f[:, None] - f[None, :]) <= SMOOTH).astype(np.float32)
    counts = inside.sum(axis=1)
    return np.tile(inside, (1, 2)).astype(ml_dtypes.bfloat16), (1.0 / counts)[:, None].astype(np.float32)


def dot(a, b):
    return math.fsum(p * q for p, q in zip(a, b))


def row_basis(rows, count):
    left = [list(r) for r in rows]
    basis = []
    for _ in range(count):
        norms = [dot(r, r) for r in left]
        best = max(range(len(left)), key=lambda i: norms[i])
        q = left[best]
        for _ in range(2):
            for b in basis:
                d = dot(q, b)
                q = [x - d * y for x, y in zip(q, b)]
            size = math.sqrt(dot(q, q))
            q = [x / size for x in q]
        basis.append(q)
        for i, r in enumerate(left):
            d = dot(r, q)
            left[i] = [x - d * y for x, y in zip(r, q)]
    return basis


@functools.cache
def lag_factors(windows):
    factor = 1.0 / math.sqrt(BINS * windows)
    mid = LAGS // 2
    bins = range(BIN0, BIN0 + BINS)

    def angle(tau, k):
        return 2.0 * math.pi / WINLEN * (tau * k % WINLEN)

    even = [[math.cos(angle(t, k)) for k in bins] for t in range(mid + 1)]
    odd = [[-math.sin(angle(t, k)) for k in bins] for t in range(1, mid + 1)]
    even_basis = row_basis(even, HALF_RANK)
    odd_basis = row_basis(odd, HALF_RANK)
    even_u = np.array([[dot(r, b) for b in even_basis] for r in even])
    odd_u = np.array([[dot(r, b) for b in odd_basis] for r in odd])
    u = np.zeros((LAGS, RANK))
    for t in range(LAGS):
        tau = t - mid
        u[t, :HALF_RANK] = even_u[abs(tau)]
        if tau:
            u[t, HALF_RANK:] = math.copysign(1.0, tau) * odd_u[abs(tau) - 1]
    return u * factor, np.array(even_basis), np.array(odd_basis)


def split_bf16(value):
    high = value.astype(np.float32).astype(ml_dtypes.bfloat16)
    low = (value - high.astype(np.float64)).astype(np.float32).astype(ml_dtypes.bfloat16)
    return high, low


def bin_order():
    order = []
    for j in range(32):
        x, z, y = j // 8, j // 2 % 4, j % 2
        order += [2 * j, 2 * j + 1]
        order += [64 + 2 * ((z * 4 + x) * 2 + y), 65 + 2 * ((z * 4 + x) * 2 + y)]
    return np.array(order)


def spectra_kernel(chunk, x_ref, next_ref, edge_ref, table_ref, band_ref, inverse_ref, out_ref, rows):
    i = pl.program_id(0)
    tail = jnp.where(i == pl.num_programs(0) - 1, edge_ref[...], next_ref[...])
    pairs = range(chunk // 2)
    spectra, magnitudes, parts = [], [], []
    for pair in pairs:
        frames = []
        for w in (2 * pair, 2 * pair + 1):
            if w == chunk - 1:
                frames.append(jnp.concatenate([x_ref[:, w * HOP :], tail], axis=1))
            else:
                frames.append(x_ref[:, w * HOP : w * HOP + WINLEN])
        spectra.append(
            lax.dot_general(
                table_ref[...],
                jnp.concatenate(frames, axis=0),
                (((1,), (1,)), ((), ())),
                preferred_element_type=jnp.float32,
            )
        )
    for value in spectra:
        re, im = value[:BINS], value[BINS:]
        magnitude = jnp.sqrt(re * re + im * im + magnitude_eps)
        high = magnitude.astype(jnp.bfloat16)
        low = (magnitude - high.astype(jnp.float32)).astype(jnp.bfloat16)
        magnitudes.append(magnitude)
        parts.append(jnp.concatenate([high, low], axis=0))
    totals = [jnp.dot(band_ref[...], p, preferred_element_type=jnp.float32) for p in parts]
    for pair in pairs:
        mean = jnp.sum(magnitudes[pair], axis=0, keepdims=True) * (1.0 / BINS)
        scale = 1.0 / (totals[pair] * inverse_ref[...] + water_level * mean)
        for part in range(2):
            white = spectra[pair][part * BINS : (part + 1) * BINS] * scale
            for h in range(2):
                row = part * chunk + 2 * pair + h
                rows[pl.ds(row, BINS, stride=2 * chunk), :] = white[:, h * 128 : (h + 1) * 128]
    for q, f in enumerate(bin_order()):
        out_ref[q] = rows[2 * chunk * int(f) : 2 * chunk * (int(f) + 1), :].astype(jnp.bfloat16)


def whitened_spectra(samples, edge):
    channels, length = samples.shape
    windows = length // HOP
    band, inverse = band_tables()
    whole = lambda shape: pl.BlockSpec(shape, lambda i: (0,) * len(shape))
    return pl.pallas_call(
        functools.partial(spectra_kernel, GROUP),
        grid=(windows // GROUP,),
        out_shape=jax.ShapeDtypeStruct((BINS, 2 * windows, channels), jnp.bfloat16),
        in_specs=[
            pl.BlockSpec((channels, GROUP * HOP), lambda i: (0, i)),
            pl.BlockSpec((channels, HOP), lambda i: (0, jnp.minimum((i + 1) * GROUP, windows - 1))),
            whole((channels, HOP)),
            whole((2 * BINS, WINLEN)),
            whole((BINS, 2 * BINS)),
            whole((BINS, 1)),
        ],
        out_specs=pl.BlockSpec((BINS, 2 * GROUP, channels), lambda i: (0, i, 0)),
        scratch_shapes=[pltpu.VMEM((BINS * 2 * GROUP, channels), jnp.float32)],
        compiler_params=pltpu.CompilerParams(vmem_limit_bytes=VMEM_BYTES),
        name="spectra",
    )(samples, samples, edge, jnp.asarray(dft_table()), jnp.asarray(band), jnp.asarray(inverse))


def add_cross(spans, pieces, slots, base, row, real_rows, imag_rows):
    results = []
    for piece, size in pieces:
        for j in range(size):
            slot = slots[base + len(results)]
            width = piece.shape[-1] // len(spans)
            total = None
            for n, span in enumerate(spans):
                own = span(slot)
                turned = []
                for r in range(0, own.shape[0], 2 * GROUP):
                    turned += [own[r + GROUP : r + 2 * GROUP], -own[r : r + GROUP]]
                cross = lax.dot_general(
                    piece[0, j][:, n * width : (n + 1) * width],
                    jnp.concatenate([own, jnp.concatenate(turned, axis=0)], axis=1),
                    (((0,), (0,)), ((), ())),
                    preferred_element_type=jnp.float32,
                )
                total = cross if total is None else total + cross
            results.append(total)
    for j, cross in enumerate(results):
        real_rows[pl.ds(base + j, cross.shape[0], stride=row), :] = cross[:, :128]
        imag_rows[pl.ds(base + j, cross.shape[0], stride=row), :] = cross[:, 128:]


def coefficients(v_ref, real_rows, imag_rows, row, bins, channels):
    results = []
    for n in range(0, len(channels), 2):
        halves = []
        for b in channels[n : n + 2]:
            start = pl.multiple_of(b * row, 8)
            halves.append(
                jnp.concatenate(
                    [real_rows[pl.ds(start, bins), :], imag_rows[pl.ds(start, bins), :]], axis=0
                ).astype(jnp.bfloat16)
            )
        results.append(jnp.dot(v_ref[...], jnp.concatenate(halves, axis=1), preferred_element_type=jnp.float32))
    totals = []
    for both in results:
        total = both[:RANK] + both[RANK:]
        totals += [total[:, :128], total[:, 128:]]
    return totals


def both_spans(own_ref, across_refs):
    middle = own_ref.shape[1] // 2
    return [
        lambda slot, start=start, across=across: jnp.concatenate(
            [own_ref[slot, start : start + middle], across[slot]], axis=0
        )
        for start, across in zip((0, middle), across_refs)
    ]


def halves_of(planes):
    return [(plane.at[half], plane.shape[2]) for plane in planes for half in range(2)]


def near_kernel(count, slots_ref, v_ref, own_ref, upper_ref, lower_ref, *refs):
    pieces, (out_ref, real_rows, imag_rows) = refs[:count], refs[count:]
    spans = both_spans(own_ref, (upper_ref, lower_ref))
    size = pieces[0].shape[2]
    bins = 2 * count * size
    row = bins + 8
    for n in range(0, count, 2):
        add_cross(spans, halves_of(pieces[n : n + 2]), slots_ref, 2 * n * size, row, real_rows, imag_rows)

    def some(n, carry):
        channels = [n * 32 + j for j in range(32)]
        totals = coefficients(v_ref, real_rows, imag_rows, row, bins, channels)
        for b, total in zip(channels, totals):
            out_ref[0, b] = total
        return carry

    lax.fori_loop(0, 2, some, 0)


def far_kernel(count, slots_ref, v_ref, own_hbm, upper_hbm, lower_hbm, near_ref, *refs):
    pieces, refs = refs[:count], refs[count:]
    keep_ref, send_ref, own_ref, upper_ref, lower_ref, real_rows, imag_rows, sems = refs
    size = pieces[0].shape[1]
    bins = count * size
    row = bins + 8

    @pl.when(pl.program_id(0) == 0)
    def _():
        copies = []
        for n, (source, target) in enumerate(((own_hbm, own_ref), (upper_hbm, upper_ref), (lower_hbm, lower_ref))):
            copies += [
                pltpu.make_async_copy(source.at[slots_ref[j]], target.at[j], sems.at[n * bins + j])
                for j in range(bins)
            ]
        for copy in copies:
            copy.start()
        for copy in copies:
            copy.wait()

    spans = both_spans(own_ref, (upper_ref, lower_ref))
    add_cross(spans, [(p, size) for p in pieces], range(bins), 0, row, real_rows, imag_rows)
    core = slots_ref[bins]
    for out_ref, which in ((send_ref, 1 - core), (keep_ref, core)):
        channels = [which * 32 + j for j in range(32)]
        totals = coefficients(v_ref, real_rows, imag_rows, row, bins, channels)
        for j, total in enumerate(totals):
            out_ref[0, j] = (near_ref[0, channels[j]] + total).astype(out_ref.dtype)


def step_block(shape):
    return pl.BlockSpec((1,) + shape, lambda s: (s,) + (0,) * len(shape))


def near_coefficients(own, across, pieces, slots, v):
    bins = sum(p.shape[0] * p.shape[2] for p in pieces)
    whole = lambda a: pl.BlockSpec(a.shape, lambda s: (0,) * a.ndim)
    return pl.pallas_call(
        functools.partial(near_kernel, len(pieces)),
        grid=(STEPS,),
        out_shape=jax.ShapeDtypeStruct((STEPS, 64, RANK, 128), jnp.float32),
        in_specs=[pl.BlockSpec(memory_space=pltpu.SMEM), whole(v), whole(own)]
        + [whole(a) for a in across]
        + [pl.BlockSpec((2, 1) + p.shape[2:], lambda s: (0, s, 0, 0, 0)) for p in pieces],
        out_specs=step_block((64, RANK, 128)),
        scratch_shapes=[pltpu.VMEM((64 * (bins + 8), 128), jnp.float32)] * 2,
        compiler_params=pltpu.CompilerParams(vmem_limit_bytes=VMEM_BYTES),
        name="near",
    )(slots, v, own, *across, *pieces)


def all_coefficients(own, across, near, pieces, slots, v):
    hbm = pl.BlockSpec(memory_space=pl.ANY)
    bins = sum(p.shape[1] for p in pieces)
    rows = (32, RANK, 128)
    return pl.pallas_call(
        functools.partial(far_kernel, len(pieces)),
        grid=(STEPS,),
        out_shape=[
            jax.ShapeDtypeStruct((STEPS,) + rows, jnp.float32),
            jax.ShapeDtypeStruct((STEPS,) + rows, jnp.bfloat16),
        ],
        in_specs=[pl.BlockSpec(memory_space=pltpu.SMEM), pl.BlockSpec(v.shape, lambda s: (0, 0))]
        + [hbm] * 3
        + [step_block(a.shape[1:]) for a in [near] + pieces],
        out_specs=[step_block(rows)] * 2,
        scratch_shapes=[pltpu.VMEM((bins,) + a.shape[1:], jnp.bfloat16) for a in (own,) + across]
        + [pltpu.VMEM((64 * (bins + 8), 128), jnp.float32)] * 2
        + [pltpu.SemaphoreType.DMA((3 * bins,))],
        compiler_params=pltpu.CompilerParams(vmem_limit_bytes=VMEM_BYTES),
        name="far",
    )(slots, v, own, *across, near, *pieces)


def expand_kernel(u_ref, keep_ref, got_ref, out_ref):
    count = keep_ref.shape[1]
    results = []
    for n in range(0, count, 2):
        value = jnp.concatenate([keep_ref[0, b] + got_ref[0, b].astype(jnp.float32) for b in (n, n + 1)], axis=1)
        high = value.astype(jnp.bfloat16)
        low = (value - high.astype(jnp.float32)).astype(jnp.bfloat16)
        results.append(
            jnp.dot(u_ref[...], jnp.concatenate([high, high, low], axis=0), preferred_element_type=jnp.float32)
        )
    for n, lags in enumerate(results):
        out_ref[0, pl.ds(2 * n, LAGS, stride=count), :] = lags[:LAGS, :128]
        out_ref[0, pl.ds(2 * n + 1, LAGS, stride=count), :] = lags[:LAGS, 128:]


def expand(u, keep, got):
    shape = (LAGS * keep.shape[1], 128)
    return pl.pallas_call(
        expand_kernel,
        grid=(STEPS,),
        out_shape=jax.ShapeDtypeStruct((STEPS,) + shape, jnp.float32),
        in_specs=[pl.BlockSpec(u.shape, lambda s: (0, 0)), step_block(keep.shape[1:]), step_block(got.shape[1:])],
        out_specs=step_block(shape),
        compiler_params=pltpu.CompilerParams(vmem_limit_bytes=VMEM_BYTES),
        name="expand",
    )(u, keep, got)


def place(x, z, y):
    return (x % 4) * 8 + (z % 4) * 2 + y % 2


def shift(value, dx=0, dz=0, dy=0):
    pairs = [(place(x, z, y), place(x + dx, z + dz, y + dy)) for x in range(4) for z in range(4) for y in range(2)]
    return lax.ppermute(value, "chan", pairs)


def plane(own, axis):
    ahead, behind, far = [shift(own, **{axis: step}) for step in (1, -1, 2)]
    return jnp.stack([jnp.concatenate([own, ahead], axis=1), jnp.concatenate([behind, far], axis=1)])


def gather_planes(parts):
    pairs = [(4 * c + t, 4 * (c ^ 1) + (t ^ 2)) for c in range(32) for t in range(4)]
    middle, columns = parts.shape[2] // 2, parts.shape[3] // 2
    lower = lax.axis_index("tm") < 2
    sides = parts[..., :columns], parts[..., columns:]

    def packed(side):
        return jnp.concatenate([side[:, :, :middle], side[:, :, middle:]], axis=3)

    mine = packed(jnp.where(lower, sides[0], sides[1]))
    theirs = packed(jnp.where(lower, sides[1], sides[0]))
    beside = shift(mine, dy=1)
    beyond = from_other_chip(theirs)
    across = lax.ppermute(theirs, ("chan", "tm"), pairs)
    own = jnp.concatenate([mine, beyond], axis=2)
    other = jnp.concatenate([beside, across], axis=2)
    first = jnp.concatenate([own[:, :2], other[:, :2]], axis=1)
    second = jnp.concatenate([own[:, 2:], other[:, 2:]], axis=1)
    return lax.optimization_barrier((first, second))


def plane_slots(last):
    me = lax.axis_index("chan")
    x, z, y = me // 8, me // 2 % 4, me % 2
    plane, dy, e = np.meshgrid(np.array((0, -1, 1, 2)), np.arange(2), np.arange(2), indexing="ij")
    plane, dy, e = (t.reshape(-1).astype(np.int32) for t in (plane, dy, e))
    y_of = (y + dy) % 2
    first = (((x + last + 4) % 4) * 8 + ((z + plane + 4) % 4) * 2 + y_of) * 4 + e
    second = (((x + plane + 4) % 4) * 8 + ((z + last + 4) % 4) * 2 + y_of) * 4 + 2 + e
    return [first, second]


def from_other_core(value):
    return lax.ppermute(value, "tm", [(0, 1), (1, 0), (2, 3), (3, 2)])


def from_other_chip(value):
    return lax.ppermute(value, "tm", [(0, 2), (2, 0), (1, 3), (3, 1)])


def basis_columns(windows, slots):
    _, even, odd = lag_factors(windows)
    parts = [split_bf16(t[:, bin_order()]) for t in (even, odd)]
    table = np.concatenate([parts[0][0], parts[1][0], parts[0][1], parts[1][1]], axis=0)
    chosen = (jnp.arange(BINS, dtype=jnp.int32)[:, None] == slots[None, :]).astype(jnp.bfloat16)
    table = jnp.dot(jnp.asarray(table), chosen, preferred_element_type=jnp.float32).astype(jnp.bfloat16)
    is_odd = (np.arange(2 * RANK) // HALF_RANK % 2 == 1)[:, None]
    nothing = jnp.zeros_like(table)
    real, imag = jnp.where(is_odd, nothing, table), jnp.where(is_odd, table, nothing)
    return lambda start, stop: jnp.concatenate([real[:, start:stop], imag[:, start:stop]], axis=1)


def shards(samples, plan, owner_table):
    windows = samples.shape[1] // HOP * lax.axis_size("tm")
    edge = lax.ppermute(samples[:, :HOP], "tm", [(1, 0), (2, 1), (3, 2)])
    own = whitened_spectra(samples, edge)
    slots = jnp.concatenate(sum([plane_slots(last) for last in (0, -1, 1, 2)], [])).astype(jnp.int32)
    v = basis_columns(windows, slots)
    core = (lax.axis_index("tm") % 2).astype(jnp.int32)[None]
    near_bins = BINS * 3 // 4
    padded = np.zeros((104, RANK))
    padded[:LAGS] = lag_factors(windows)[0]
    high, low = split_bf16(padded)
    u = jnp.asarray(np.concatenate([high, low, high], axis=1))
    tables = (slots[:near_bins], jnp.concatenate([slots[near_bins:], core]), v(0, near_bins), v(near_bins, BINS))
    everyone = lax.all_to_all(own.reshape((32, 4) + own.shape[1:]), "chan", 0, 0)
    middle = own.shape[1] // 2
    leaving = own[:, :middle], own[:, middle:]
    everyone, tables, leaving = lax.optimization_barrier((everyone, tables, leaving))
    upper = from_other_chip(leaving[0])
    near_slots, far_slots, near_v, far_v = tables
    roots = owner_table[plan]
    parts = jnp.stack([lax.dynamic_index_in_dim(everyone, roots[s], 0, keepdims=False) for s in range(STEPS)])
    first, second = gather_planes(parts)
    plane_a, plane_b = plane(first, "dz"), plane(second, "dx")
    plane_b, upper, lower = lax.optimization_barrier((plane_b, upper, leaving[1]))
    across = upper, from_other_chip(lower)
    near = [
        shift(plane_a, dx=1),
        shift(plane_b, dz=1),
        shift(plane_a, dx=-1),
        shift(plane_b, dz=-1),
    ]
    far = [
        shift(near[0][0], dx=1),
        shift(near[2][1], dx=-1),
        shift(near[1][0], dz=1),
        shift(near[3][1], dz=-1),
    ]
    partial = near_coefficients(own, across, [plane_a, plane_b] + near, near_slots, near_v)
    far, partial = lax.optimization_barrier((far, partial))
    keep, send = all_coefficients(own, across, partial, far, far_slots, far_v)
    out = expand(u, keep, from_other_core(send))
    return out.reshape(STEPS, LAGS, 32, 128).transpose(2, 0, 1, 3)


def solution(mesh):
    placed = (P("chan", "tm"), P(), P())
    return jax.shard_map(
        shards, mesh=mesh, in_specs=placed, out_specs=P("tm", None, None, "chan"), check_vma=False
    )
```

```python
import functools
import math

import jax
import jax.numpy as jnp
import ml_dtypes
import numpy as np
from jax import lax
from jax.experimental import pallas as pl
from jax.experimental.pallas import tpu as pltpu
from jax.sharding import PartitionSpec as P

WINLEN = 1024
HOP = 512
BINS = 128
BIN0 = 16
SMOOTH = 4
LAGS = 101
STEPS = 3
HALF_RANK = 24
RANK = 2 * HALF_RANK
GROUP = 8
magnitude_eps = 1e-06
water_level = 0.25
VMEM_BYTES = 60 * 1024 * 1024


def dft_table():
    n = np.arange(WINLEN)
    k = BIN0 + np.arange(BINS)
    angles = 2.0 * math.pi / WINLEN * (k[:, None] * n[None, :] % WINLEN)
    taper = 0.5 - 0.5 * np.cos(2.0 * math.pi / WINLEN * n)
    table = np.concatenate([np.cos(angles) * taper, -np.sin(angles) * taper], axis=0)
    return table.astype(np.float32).astype(ml_dtypes.bfloat16)


def band_tables():
    f = np.arange(BINS)
    inside = (np.abs(f[:, None] - f[None, :]) <= SMOOTH).astype(np.float32)
    counts = inside.sum(axis=1)
    return np.tile(inside, (1, 2)).astype(ml_dtypes.bfloat16), (1.0 / counts)[:, None].astype(np.float32)


def dot(a, b):
    return math.fsum(p * q for p, q in zip(a, b))


def row_basis(rows, count):
    left = [list(r) for r in rows]
    basis = []
    for _ in range(count):
        norms = [dot(r, r) for r in left]
        best = max(range(len(left)), key=lambda i: norms[i])
        q = left[best]
        for _ in range(2):
            for b in basis:
                d = dot(q, b)
                q = [x - d * y for x, y in zip(q, b)]
            size = math.sqrt(dot(q, q))
            q = [x / size for x in q]
        basis.append(q)
        for i, r in enumerate(left):
            d = dot(r, q)
            left[i] = [x - d * y for x, y in zip(r, q)]
    return basis


@functools.cache
def lag_factors(windows):
    factor = 1.0 / math.sqrt(BINS * windows)
    mid = LAGS // 2
    bins = range(BIN0, BIN0 + BINS)

    def angle(tau, k):
        return 2.0 * math.pi / WINLEN * (tau * k % WINLEN)

    even = [[math.cos(angle(t, k)) for k in bins] for t in range(mid + 1)]
    odd = [[-math.sin(angle(t, k)) for k in bins] for t in range(1, mid + 1)]
    even_basis = row_basis(even, HALF_RANK)
    odd_basis = row_basis(odd, HALF_RANK)
    even_u = np.array([[dot(r, b) for b in even_basis] for r in even])
    odd_u = np.array([[dot(r, b) for b in odd_basis] for r in odd])
    u = np.zeros((LAGS, RANK))
    for t in range(LAGS):
        tau = t - mid
        u[t, :HALF_RANK] = even_u[abs(tau)]
        if tau:
            u[t, HALF_RANK:] = math.copysign(1.0, tau) * odd_u[abs(tau) - 1]
    return u * factor, np.array(even_basis), np.array(odd_basis)


def split_bf16(value):
    high = value.astype(np.float32).astype(ml_dtypes.bfloat16)
    low = (value - high.astype(np.float64)).astype(np.float32).astype(ml_dtypes.bfloat16)
    return high, low


def bin_order():
    order = []
    for j in range(32):
        x, z, y = j // 8, j // 2 % 4, j % 2
        order += [2 * j, 2 * j + 1]
        order += [64 + 2 * ((z * 4 + x) * 2 + y), 65 + 2 * ((z * 4 + x) * 2 + y)]
    return np.array(order)


def spectra_kernel(chunk, x_ref, next_ref, edge_ref, table_ref, band_ref, inverse_ref, out_ref, rows):
    i = pl.program_id(0)
    tail = jnp.where(i == pl.num_programs(0) - 1, edge_ref[...], next_ref[...])
    pairs = range(chunk // 2)
    spectra, magnitudes, parts = [], [], []
    for pair in pairs:
        frames = []
        for w in (2 * pair, 2 * pair + 1):
            if w == chunk - 1:
                frames.append(jnp.concatenate([x_ref[:, w * HOP :], tail], axis=1))
            else:
                frames.append(x_ref[:, w * HOP : w * HOP + WINLEN])
        spectra.append(
            lax.dot_general(
                table_ref[...],
                jnp.concatenate(frames, axis=0),
                (((1,), (1,)), ((), ())),
                preferred_element_type=jnp.float32,
            )
        )
    for value in spectra:
        re, im = value[:BINS], value[BINS:]
        magnitude = jnp.sqrt(re * re + im * im + magnitude_eps)
        high = magnitude.astype(jnp.bfloat16)
        low = (magnitude - high.astype(jnp.float32)).astype(jnp.bfloat16)
        magnitudes.append(magnitude)
        parts.append(jnp.concatenate([high, low], axis=0))
    totals = [jnp.dot(band_ref[...], p, preferred_element_type=jnp.float32) for p in parts]
    for pair in pairs:
        mean = jnp.sum(magnitudes[pair], axis=0, keepdims=True) * (1.0 / BINS)
        scale = 1.0 / (totals[pair] * inverse_ref[...] + water_level * mean)
        for part in range(2):
            white = spectra[pair][part * BINS : (part + 1) * BINS] * scale
            for h in range(2):
                row = part * chunk + 2 * pair + h
                rows[pl.ds(row, BINS, stride=2 * chunk), :] = white[:, h * 128 : (h + 1) * 128]
    for q, f in enumerate(bin_order()):
        out_ref[q] = rows[2 * chunk * int(f) : 2 * chunk * (int(f) + 1), :].astype(jnp.bfloat16)


def whitened_spectra(samples, edge):
    channels, length = samples.shape
    windows = length // HOP
    band, inverse = band_tables()
    whole = lambda shape: pl.BlockSpec(shape, lambda i: (0,) * len(shape))
    return pl.pallas_call(
        functools.partial(spectra_kernel, GROUP),
        grid=(windows // GROUP,),
        out_shape=jax.ShapeDtypeStruct((BINS, 2 * windows, channels), jnp.bfloat16),
        in_specs=[
            pl.BlockSpec((channels, GROUP * HOP), lambda i: (0, i)),
            pl.BlockSpec((channels, HOP), lambda i: (0, jnp.minimum((i + 1) * GROUP, windows - 1))),
            whole((channels, HOP)),
            whole((2 * BINS, WINLEN)),
            whole((BINS, 2 * BINS)),
            whole((BINS, 1)),
        ],
        out_specs=pl.BlockSpec((BINS, 2 * GROUP, channels), lambda i: (0, i, 0)),
        scratch_shapes=[pltpu.VMEM((BINS * 2 * GROUP, channels), jnp.float32)],
        compiler_params=pltpu.CompilerParams(vmem_limit_bytes=VMEM_BYTES),
        name="spectra",
    )(samples, samples, edge, jnp.asarray(dft_table()), jnp.asarray(band), jnp.asarray(inverse))


def add_cross(spans, pieces, slots, base, row, real_rows, imag_rows):
    results = []
    for piece, size in pieces:
        for j in range(size):
            slot = slots[base + len(results)]
            width = piece.shape[-1] // len(spans)
            total = None
            for n, span in enumerate(spans):
                own = span(slot)
                turned = []
                for r in range(0, own.shape[0], 2 * GROUP):
                    turned += [own[r + GROUP : r + 2 * GROUP], -own[r : r + GROUP]]
                cross = lax.dot_general(
                    piece[0, j][:, n * width : (n + 1) * width],
                    jnp.concatenate([own, jnp.concatenate(turned, axis=0)], axis=1),
                    (((0,), (0,)), ((), ())),
                    preferred_element_type=jnp.float32,
                )
                total = cross if total is None else total + cross
            results.append(total)
    for j, cross in enumerate(results):
        real_rows[pl.ds(base + j, cross.shape[0], stride=row), :] = cross[:, :128]
        imag_rows[pl.ds(base + j, cross.shape[0], stride=row), :] = cross[:, 128:]


def coefficients(v_ref, real_rows, imag_rows, row, bins, channels):
    results = []
    for n in range(0, len(channels), 2):
        halves = []
        for b in channels[n : n + 2]:
            start = pl.multiple_of(b * row, 8)
            halves.append(
                jnp.concatenate(
                    [real_rows[pl.ds(start, bins), :], imag_rows[pl.ds(start, bins), :]], axis=0
                ).astype(jnp.bfloat16)
            )
        results.append(jnp.dot(v_ref[...], jnp.concatenate(halves, axis=1), preferred_element_type=jnp.float32))
    totals = []
    for both in results:
        total = both[:RANK] + both[RANK:]
        totals += [total[:, :128], total[:, 128:]]
    return totals


def both_spans(own_ref, across_refs):
    middle = own_ref.shape[1] // 2
    return [
        lambda slot, start=start, across=across: jnp.concatenate(
            [own_ref[slot, start : start + middle], across[slot]], axis=0
        )
        for start, across in zip((0, middle), across_refs)
    ]


def halves_of(planes):
    return [(plane.at[half], plane.shape[2]) for plane in planes for half in range(2)]


def near_kernel(count, slots_ref, v_ref, own_ref, upper_ref, lower_ref, *refs):
    pieces, (out_ref, real_rows, imag_rows) = refs[:count], refs[count:]
    spans = both_spans(own_ref, (upper_ref, lower_ref))
    size = pieces[0].shape[2]
    bins = 2 * count * size
    row = bins + 8
    for n in range(0, count, 2):
        add_cross(spans, halves_of(pieces[n : n + 2]), slots_ref, 2 * n * size, row, real_rows, imag_rows)

    def some(n, carry):
        channels = [n * 32 + j for j in range(32)]
        totals = coefficients(v_ref, real_rows, imag_rows, row, bins, channels)
        for b, total in zip(channels, totals):
            out_ref[0, b] = total.astype(out_ref.dtype)
        return carry

    lax.fori_loop(0, 2, some, 0)


def far_kernel(count, slots_ref, v_ref, own_hbm, upper_hbm, lower_hbm, near_ref, *refs):
    pieces, refs = refs[:count], refs[count:]
    keep_ref, send_ref, own_ref, upper_ref, lower_ref, real_rows, imag_rows, sems = refs
    size = pieces[0].shape[1]
    bins = count * size
    row = bins + 8

    @pl.when(pl.program_id(0) == 0)
    def _():
        copies = []
        for n, (source, target) in enumerate(((own_hbm, own_ref), (upper_hbm, upper_ref), (lower_hbm, lower_ref))):
            copies += [
                pltpu.make_async_copy(source.at[slots_ref[j]], target.at[j], sems.at[n * bins + j])
                for j in range(bins)
            ]
        for copy in copies:
            copy.start()
        for copy in copies:
            copy.wait()

    spans = both_spans(own_ref, (upper_ref, lower_ref))
    add_cross(spans, [(p, size) for p in pieces], range(bins), 0, row, real_rows, imag_rows)
    core = slots_ref[bins]
    for out_ref, which in ((send_ref, 1 - core), (keep_ref, core)):
        channels = [which * 32 + j for j in range(32)]
        totals = coefficients(v_ref, real_rows, imag_rows, row, bins, channels)
        for j, total in enumerate(totals):
            out_ref[0, j] = (near_ref[0, channels[j]].astype(jnp.float32) + total).astype(out_ref.dtype)


def step_block(shape):
    return pl.BlockSpec((1,) + shape, lambda s: (s,) + (0,) * len(shape))


def near_coefficients(own, across, pieces, slots, v):
    bins = sum(p.shape[0] * p.shape[2] for p in pieces)
    whole = lambda a: pl.BlockSpec(a.shape, lambda s: (0,) * a.ndim)
    return pl.pallas_call(
        functools.partial(near_kernel, len(pieces)),
        grid=(STEPS,),
        out_shape=jax.ShapeDtypeStruct((STEPS, 64, RANK, 128), jnp.bfloat16),
        in_specs=[pl.BlockSpec(memory_space=pltpu.SMEM), whole(v), whole(own)]
        + [whole(a) for a in across]
        + [pl.BlockSpec((2, 1) + p.shape[2:], lambda s: (0, s, 0, 0, 0)) for p in pieces],
        out_specs=step_block((64, RANK, 128)),
        scratch_shapes=[pltpu.VMEM((64 * (bins + 8), 128), jnp.float32)] * 2,
        compiler_params=pltpu.CompilerParams(vmem_limit_bytes=VMEM_BYTES),
        name="near",
    )(slots, v, own, *across, *pieces)


def all_coefficients(own, across, near, pieces, slots, v):
    hbm = pl.BlockSpec(memory_space=pl.ANY)
    bins = sum(p.shape[1] for p in pieces)
    rows = (32, RANK, 128)
    return pl.pallas_call(
        functools.partial(far_kernel, len(pieces)),
        grid=(STEPS,),
        out_shape=[
            jax.ShapeDtypeStruct((STEPS,) + rows, jnp.bfloat16),
            jax.ShapeDtypeStruct((STEPS,) + rows, jnp.bfloat16),
        ],
        in_specs=[pl.BlockSpec(memory_space=pltpu.SMEM), pl.BlockSpec(v.shape, lambda s: (0, 0))]
        + [hbm] * 3
        + [step_block(a.shape[1:]) for a in [near] + pieces],
        out_specs=[step_block(rows)] * 2,
        scratch_shapes=[pltpu.VMEM((bins,) + a.shape[1:], jnp.bfloat16) for a in (own,) + across]
        + [pltpu.VMEM((64 * (bins + 8), 128), jnp.float32)] * 2
        + [pltpu.SemaphoreType.DMA((3 * bins,))],
        compiler_params=pltpu.CompilerParams(vmem_limit_bytes=VMEM_BYTES),
        name="far",
    )(slots, v, own, *across, near, *pieces)


def expand_kernel(u_ref, keep_ref, got_ref, out_ref):
    count = keep_ref.shape[1]
    results = []
    for n in range(0, count, 2):
        value = jnp.concatenate([keep_ref[0, b].astype(jnp.float32) + got_ref[0, b].astype(jnp.float32) for b in (n, n + 1)], axis=1)
        high = value.astype(jnp.bfloat16)
        low = (value - high.astype(jnp.float32)).astype(jnp.bfloat16)
        results.append(
            jnp.dot(u_ref[...], jnp.concatenate([high, high, low], axis=0), preferred_element_type=jnp.float32)
        )
    for n, lags in enumerate(results):
        out_ref[0, pl.ds(2 * n, LAGS, stride=count), :] = lags[:LAGS, :128]
        out_ref[0, pl.ds(2 * n + 1, LAGS, stride=count), :] = lags[:LAGS, 128:]


def expand(u, keep, got):
    shape = (LAGS * keep.shape[1], 128)
    return pl.pallas_call(
        expand_kernel,
        grid=(STEPS,),
        out_shape=jax.ShapeDtypeStruct((STEPS,) + shape, jnp.float32),
        in_specs=[pl.BlockSpec(u.shape, lambda s: (0, 0)), step_block(keep.shape[1:]), step_block(got.shape[1:])],
        out_specs=step_block(shape),
        compiler_params=pltpu.CompilerParams(vmem_limit_bytes=VMEM_BYTES),
        name="expand",
    )(u, keep, got)


def place(x, z, y):
    return (x % 4) * 8 + (z % 4) * 2 + y % 2


def shift(value, dx=0, dz=0, dy=0):
    pairs = [(place(x, z, y), place(x + dx, z + dz, y + dy)) for x in range(4) for z in range(4) for y in range(2)]
    return lax.ppermute(value, "chan", pairs)


def plane(own, axis):
    ahead, behind, far = [shift(own, **{axis: step}) for step in (1, -1, 2)]
    return jnp.stack([jnp.concatenate([own, ahead], axis=1), jnp.concatenate([behind, far], axis=1)])


def gather_planes(parts):
    pairs = [(4 * c + t, 4 * (c ^ 1) + (t ^ 2)) for c in range(32) for t in range(4)]
    middle, columns = parts.shape[2] // 2, parts.shape[3] // 2
    lower = lax.axis_index("tm") < 2
    sides = parts[..., :columns], parts[..., columns:]

    def packed(side):
        return jnp.concatenate([side[:, :, :middle], side[:, :, middle:]], axis=3)

    mine = packed(jnp.where(lower, sides[0], sides[1]))
    theirs = packed(jnp.where(lower, sides[1], sides[0]))
    beside = shift(mine, dy=1)
    beyond = from_other_chip(theirs)
    across = lax.ppermute(theirs, ("chan", "tm"), pairs)
    own = jnp.concatenate([mine, beyond], axis=2)
    other = jnp.concatenate([beside, across], axis=2)
    first = jnp.concatenate([own[:, :2], other[:, :2]], axis=1)
    second = jnp.concatenate([own[:, 2:], other[:, 2:]], axis=1)
    return lax.optimization_barrier((first, second))


def plane_slots(last):
    me = lax.axis_index("chan")
    x, z, y = me // 8, me // 2 % 4, me % 2
    plane, dy, e = np.meshgrid(np.array((0, -1, 1, 2)), np.arange(2), np.arange(2), indexing="ij")
    plane, dy, e = (t.reshape(-1).astype(np.int32) for t in (plane, dy, e))
    y_of = (y + dy) % 2
    first = (((x + last + 4) % 4) * 8 + ((z + plane + 4) % 4) * 2 + y_of) * 4 + e
    second = (((x + plane + 4) % 4) * 8 + ((z + last + 4) % 4) * 2 + y_of) * 4 + 2 + e
    return [first, second]


def from_other_core(value):
    return lax.ppermute(value, "tm", [(0, 1), (1, 0), (2, 3), (3, 2)])


def from_other_chip(value):
    return lax.ppermute(value, "tm", [(0, 2), (2, 0), (1, 3), (3, 1)])


def basis_columns(windows, slots):
    _, even, odd = lag_factors(windows)
    parts = [split_bf16(t[:, bin_order()]) for t in (even, odd)]
    table = np.concatenate([parts[0][0], parts[1][0], parts[0][1], parts[1][1]], axis=0)
    chosen = (jnp.arange(BINS, dtype=jnp.int32)[:, None] == slots[None, :]).astype(jnp.bfloat16)
    table = jnp.dot(jnp.asarray(table), chosen, preferred_element_type=jnp.float32).astype(jnp.bfloat16)
    is_odd = (np.arange(2 * RANK) // HALF_RANK % 2 == 1)[:, None]
    nothing = jnp.zeros_like(table)
    real, imag = jnp.where(is_odd, nothing, table), jnp.where(is_odd, table, nothing)
    return lambda start, stop: jnp.concatenate([real[:, start:stop], imag[:, start:stop]], axis=1)


def shards(samples, plan, owner_table):
    windows = samples.shape[1] // HOP * lax.axis_size("tm")
    edge = lax.ppermute(samples[:, :HOP], "tm", [(1, 0), (2, 1), (3, 2)])
    own = whitened_spectra(samples, edge)
    slots = jnp.concatenate(sum([plane_slots(last) for last in (0, -1, 1, 2)], [])).astype(jnp.int32)
    v = basis_columns(windows, slots)
    core = (lax.axis_index("tm") % 2).astype(jnp.int32)[None]
    near_bins = BINS * 3 // 4
    padded = np.zeros((104, RANK))
    padded[:LAGS] = lag_factors(windows)[0]
    high, low = split_bf16(padded)
    u = jnp.asarray(np.concatenate([high, low, high], axis=1))
    tables = (slots[:near_bins], jnp.concatenate([slots[near_bins:], core]), v(0, near_bins), v(near_bins, BINS))
    everyone = lax.all_to_all(own.reshape((32, 4) + own.shape[1:]), "chan", 0, 0)
    middle = own.shape[1] // 2
    leaving = own[:, :middle], own[:, middle:]
    everyone, tables, leaving = lax.optimization_barrier((everyone, tables, leaving))
    upper = from_other_chip(leaving[0])
    near_slots, far_slots, near_v, far_v = tables
    roots = owner_table[plan]
    parts = jnp.stack([lax.dynamic_index_in_dim(everyone, roots[s], 0, keepdims=False) for s in range(STEPS)])
    first, second = gather_planes(parts)
    plane_a, plane_b = plane(first, "dz"), plane(second, "dx")
    plane_b, upper, lower = lax.optimization_barrier((plane_b, upper, leaving[1]))
    across = upper, from_other_chip(lower)
    near = [
        shift(plane_a, dx=1),
        shift(plane_b, dz=1),
        shift(plane_a, dx=-1),
        shift(plane_b, dz=-1),
    ]
    far = [
        shift(near[0][0], dx=1),
        shift(near[2][1], dx=-1),
        shift(near[1][0], dz=1),
        shift(near[3][1], dz=-1),
    ]
    partial = near_coefficients(own, across, [plane_a, plane_b] + near, near_slots, near_v)
    far, partial = lax.optimization_barrier((far, partial))
    keep, send = all_coefficients(own, across, partial, far, far_slots, far_v)
    out = expand(u, keep, from_other_core(send))
    return out.reshape(STEPS, LAGS, 32, 128).transpose(2, 0, 1, 3)


def solution(mesh):
    placed = (P("chan", "tm"), P(), P())
    return jax.shard_map(
        shards, mesh=mesh, in_specs=placed, out_specs=P("tm", None, None, "chan"), check_vma=False
    )
```
